256 devices in a mesh: dp: 8 (over z), expert: 32 (over x, y, core).
Axes of the slice: x: 4, y: 4, z: 8, core: 2. Of those that a mesh axis runs over, the one named last changes fastest.
Arguments:
- policy_states: bfloat16 [32, 8, 512, 1024], P('expert', 'dp'), may hold values from -6 to 6
- row_lengths: int32 [256], P('expert'), may hold values from 1 to 512, 65536 in all
- send_order: int32 [256], P('expert'), may hold values from 0 to 7, as said below
- expert_ids: int32 [8, 32, 512, 6], P('dp', 'expert'), may hold values from 0 to 63, all different within a row; in each aligned block of 512 rows (0 to 511, 512 to 1023, ..., all dimensions but the last counted through in order) at most 54 rows name the same one
- gate_codes: int32 [8, 32, 512, 6], P('dp', 'expert'), may hold values from 1 to 15
- w_gate: bfloat16 [64, 1024, 704], P('expert'), may hold values from -0.1875 to 0.1875
- w_up: bfloat16 [64, 1024, 704], P('expert'), may hold values from -0.1875 to 0.1875
- w_down: bfloat16 [64, 704, 1024], P('expert'), may hold values from -0.625 to 0.625
Outputs:
- judged: bfloat16 [256, 512, 1024], P(('dp', 'expert'))
The draws below stay inside these ranges and needn't reach their ends.
Inputs may be any that keep to these rules, and one draw needn't show every extreme that they name: `send_order`: each aligned block of 8 entries is a permutation of 0 to 7. `expert_ids`: among the 512 token slots of one device no expert is named by more than 54 slots, and some device's slots reach 54 for some expert. `row_lengths`: the largest length is exactly 512.
All inputs are finite; a program needn't handle non-finite values. No bound on the sum of `row_lengths` on one device may be relied on, other than what follows from the above.
Results may differ from the reference program's by a relative error of at most 0.0057.
Values may be sent and summed in bfloat16 or wider, within the bound.
No kernel may reach another device: no remote copies, remote signals or barrier semaphores. Data moves between devices by JAX's collectives and lax.ppermute only.
A program may use at most 192 MiB of HBM per device.

```python
import math
import jax
import jax.numpy as jnp
import numpy as np
from jax import lax

D = 1024
FF = 704
EXPERTS = 64
TOP = 6
MAXLEN = 512
ROWS_DEV = 1
ROWS_GROUP = 8
ROWS = 256
T_DEV = 512
CAP = 54
N_DP = 8
N_EXPERT = 32


def draw_send_order(key, part):
    group_rows = ROWS_DEV * N_DP
    shard_keys = jax.random.split(key, ROWS // group_rows)
    orders = jax.vmap(lambda shard_key: jax.random.permutation(shard_key, group_rows))(shard_keys)
    return orders.reshape(ROWS).astype(jnp.int32)


def touch_ends(values, own_key, least, largest):
    place = [jax.random.randint(jax.random.fold_in(own_key, axis), (), 0, length) for axis, length in enumerate(values.shape)]
    widest = values.shape.index(max(values.shape))
    beside = place[:widest] + [(place[widest] + 1) % values.shape[widest]] + place[widest + 1:]
    return values.at[tuple(place)].set(least).at[tuple(beside)].set(largest)


def block_scale(rng, shape, pieces, low, largest):
    factor_of, own = 1.0, jax.random.fold_in(rng, 6)
    for axis_at, shards_of in pieces:
        draws = jnp.exp(jax.random.uniform(jax.random.fold_in(own, axis_at), (shards_of,), jnp.float32, low / len(pieces), largest / len(pieces)))
        factor_of = factor_of * jnp.repeat(draws, shape[axis_at] // shards_of).reshape([-1 if axis == axis_at else 1 for axis in range(len(shape))])
    return factor_of


def split_up(number_of, total, reach, skew):
    loads = [(1 << 20) // math.isqrt(grade ** skew) + 1 for grade in range(2, number_of + 1)]
    surplus, holding = total - reach - (number_of - 1), [1] * (number_of - 1)
    while surplus > 0:
        movable = [i for i in range(number_of - 1) if holding[i] < reach]
        whole, left = sum([loads[i] for i in movable]), surplus
        for i in movable:
            extra = min(reach - holding[i], max(1, left * loads[i] // whole), surplus)
            holding[i] = holding[i] + extra
            surplus = surplus - extra
    return np.array([reach] + holding)


def ragged(own_key, amount, total, most, slope):
    if amount == 2:
        one = jax.random.randint(own_key, (), max(1, total - most), min(most, total - 1) + 1)
        return jnp.stack([one, total - one])
    sizes = jnp.asarray(split_up(amount, total, most, slope), jnp.int32)
    couples = (amount - 1) // 2
    donor, receiver = sizes[1:1 + 2 * couples:2], sizes[2:2 + 2 * couples:2]
    room = jnp.minimum(donor - 1, most - receiver)
    passed = jax.random.randint(jax.random.fold_in(own_key, 1), (couples,), 0, 1 << 20) % (room + 1)
    sizes = sizes.at[1:1 + 2 * couples:2].set(donor - passed).at[2:2 + 2 * couples:2].set(receiver + passed)
    return sizes[jax.random.permutation(jax.random.fold_in(own_key, 2), amount)]


def assign_block(own_key, own, number, rows, number_of, top, most, skew):
    ranking = jax.random.permutation(own_key, number_of)
    heavy_load, ordinary = load_shares(number_of, rows * top, most, skew, True), load_shares(number_of, rows * top, most, skew, False)
    places = jnp.arange(number_of)

    def named(sizes, offset_by):
        used = int((sizes > 0).sum())
        fixed = max(1, used // 4)
        passed = fixed + (places - fixed + offset_by * (used - fixed)) % max(1, number_of - fixed)
        return jnp.zeros((number_of,), jnp.int32).at[ranking[jnp.where(places < fixed, places, passed)]].set(jnp.asarray(sizes, jnp.int32))

    sizes = jnp.where(number % 4 == 0, named(heavy_load, number // 4), named(ordinary, number - number // 4 - 1))
    mixed = jax.random.permutation(jax.random.fold_in(own, 3), number_of)
    donor, taker = mixed[0:number_of // 2 * 2:2], mixed[1:number_of // 2 * 2:2]
    slack = jnp.minimum(sizes[donor] - 1, most - sizes[taker]) // 2
    slack = jnp.where((donor == ranking[0]) | (taker == ranking[0]) | (sizes[taker] == 0), 0, jnp.maximum(slack, 0))
    passed = jax.random.randint(jax.random.fold_in(own, 4), (number_of // 2,), 0, 1 << 20) % (slack + 1)
    sizes = sizes.at[donor].add(-passed).at[taker].add(passed)
    labels = jnp.searchsorted(jnp.cumsum(sizes), jnp.arange(rows * top), side="right").astype(jnp.int32)
    table = labels.reshape(top, rows).T
    table = table[jax.random.permutation(jax.random.fold_in(own, 1), rows)]
    offset_by = jax.random.randint(jax.random.fold_in(own, 2), (rows, 1), 0, top)
    return jnp.take_along_axis(table, (jnp.arange(top)[None, :] + offset_by) % top, axis=1)


def load_shares(amount, total, limit, lean, full):
    portions = [(1 << 20) // math.isqrt(rank ** lean) + 1 for rank in range(1, amount + 1)]
    largest = limit if full else min(limit, max(-(-total // amount), total * portions[0] // sum(portions)))
    least = 1 if total - largest >= amount - 1 else 0
    counts, rest = [largest] + [least] * (amount - 1), total - largest - least * (amount - 1)
    while rest > 0:
        candidates = [i for i in range(1, amount) if counts[i] < largest] or [i for i in range(1, amount) if counts[i] < limit]
        pool, remaining = sum([portions[i] for i in candidates]), rest
        for i in candidates:
            extra = min(limit - counts[i], max(1, remaining * portions[i] // pool), rest)
            counts[i] = counts[i] + extra
            rest = rest - extra
    return np.array(counts)


def centred(own_key, shape, scale, reach, cuts=(), kind=jnp.bfloat16):
    entries = scale * jax.random.normal(own_key, shape, jnp.float32)
    if cuts:
        entries = entries * block_scale(own_key, shape, cuts, -0.22, 0.18)
    return jnp.clip(entries, -reach, reach).astype(kind)


def setup_inputs(seed: int = 0) -> dict:
    keys = jax.random.split(jax.random.key(seed), 9)
    policy_states = centred(keys[0], (N_EXPERT, ROWS_GROUP, MAXLEN, D), 1.0, 6.0, ((0, 32), (1, 8)))
    row_lengths = ragged(keys[1], ROWS, ROWS * MAXLEN // 2, MAXLEN, 2).astype(jnp.int32)
    send_order = draw_send_order(jax.random.fold_in(keys[8], 71), 0)
    expert_ids_keys = jax.random.split(jax.random.fold_in(keys[3], 1), N_DP * N_EXPERT * T_DEV // T_DEV)
    expert_ids_turns = jax.random.permutation(jax.random.fold_in(keys[3], 3), N_DP * N_EXPERT * T_DEV // T_DEV)
    expert_ids = jax.vmap(lambda own, number: assign_block(jax.random.fold_in(keys[3], 2), own, number, T_DEV, EXPERTS, TOP, CAP, 2))(expert_ids_keys, expert_ids_turns).reshape((N_DP, N_EXPERT, T_DEV, TOP))
    gate_codes = touch_ends(jax.random.randint(keys[4], (N_DP, N_EXPERT, T_DEV, TOP), 1, 16), jax.random.fold_in(keys[4], 1), 1, 15).astype(jnp.int32)
    w_gate = centred(keys[5], (EXPERTS, D, FF), D ** -0.5, 0.1875, ((0, 32),))
    w_up = centred(keys[6], (EXPERTS, D, FF), D ** -0.5, 0.1875, ((0, 32),))
    w_down = centred(keys[7], (EXPERTS, FF, D), (FF // 8) ** -0.5, 0.625, ((0, 32),))
    return dict(policy_states=policy_states, row_lengths=row_lengths, send_order=send_order, expert_ids=expert_ids, gate_codes=gate_codes, w_gate=w_gate, w_up=w_up, w_down=w_down)


def relay_rows(values, send_order):
    group_rows = ROWS_DEV * N_DP
    source_blocks = values.reshape((N_EXPERT, group_rows) + values.shape[1:])
    row_orders = send_order.reshape(N_EXPERT, group_rows)
    picked = jax.vmap(lambda source_block, row_order: source_block[row_order])(source_blocks, row_orders)
    picked = picked.reshape((N_EXPERT, N_DP, ROWS_DEV) + values.shape[1:])
    picked = jnp.swapaxes(picked, 0, 1)
    return picked.reshape(values.shape)


def reference(policy_states, row_lengths, send_order, expert_ids, gate_codes, w_gate, w_up, w_down):
    flat_states = policy_states.reshape(ROWS, MAXLEN, D)
    relaid = relay_rows(flat_states, send_order)
    relaid_len = relay_rows(row_lengths, send_order)
    tok_all = ROWS * MAXLEN
    states = relaid.reshape(tok_all, D)
    position = jnp.arange(MAXLEN, dtype=jnp.int32)
    is_live = (position[None, :] < relaid_len[:, None]).reshape(tok_all)
    route_list = expert_ids.reshape(-1).astype(jnp.int32)
    gate_code = gate_codes.reshape(tok_all, TOP).astype(jnp.float32)
    gate_share = gate_code / jnp.sum(gate_code, axis=1, keepdims=True)
    gate_flat = jnp.concatenate([gate_share.reshape(-1), jnp.zeros((1,), jnp.float32)])
    padded = jnp.concatenate([states, jnp.zeros((1, D), states.dtype)], axis=0)
    assigns = tok_all * TOP
    slot_count = N_DP * N_EXPERT * CAP

    def one_expert(combined, inputs):
        expert, gate_mat, up_mat, down_mat = inputs
        chosen = jnp.nonzero(route_list == expert, size=slot_count, fill_value=assigns)[0].astype(jnp.int32)
        targets = (chosen // TOP).astype(jnp.int32)
        gathered = padded[targets]
        gate_val = jnp.dot(gathered, gate_mat, preferred_element_type=jnp.float32)
        up_val = jnp.dot(gathered, up_mat, preferred_element_type=jnp.float32)
        hidden = (jax.nn.silu(gate_val) * up_val).astype(jnp.bfloat16)
        output = jnp.dot(hidden, down_mat, preferred_element_type=jnp.float32).astype(jnp.bfloat16)
        combined = combined.at[targets].add(gate_flat[chosen][:, None] * output.astype(jnp.float32))
        return combined, None

    start = jnp.zeros((tok_all + 1, D), jnp.float32)
    combined, unused = lax.scan(one_expert, start, (jnp.arange(EXPERTS, dtype=jnp.int32), w_gate, w_up, w_down))
    result = jnp.where(is_live[:, None], combined[:tok_all], jnp.float32(0.0)).astype(jnp.bfloat16)
    return result.reshape(ROWS, MAXLEN, D)
```

```python
import functools

import jax
import jax.numpy as jnp
from jax import lax
from jax.experimental import pallas as pl
from jax.experimental.pallas import tpu as pltpu
from jax.sharding import Mesh, PartitionSpec as P

F32 = jnp.float32
BF16 = jnp.bfloat16
I32 = jnp.int32
ALL = ("dp", "x", "y", "core")
PLANE = ("x", "y", "core")
CHUNKS = 2
BLOCK = 256
PICK = 64


def one_hot(rows, columns):
    return (rows[:, None] == columns[None, :]).astype(BF16)


def pick(matrix, values):
    return jnp.dot(matrix, values, preferred_element_type=F32).astype(BF16)


def shift(value, axis, by):
    size = lax.axis_size(axis)
    return lax.ppermute(value, axis, [(i, (i + by) % size) for i in range(size)])


def ring_sum(value, axis):
    rows = value.shape[0] // 4
    half = rows // 2
    own, after, across, before = (value[i * rows : (i + 1) * rows] for i in range(4))
    low = shift(across[:half], axis, -1)
    high = shift(across[half:], axis, 1)
    before = jnp.concatenate(
        [(before[:half].astype(F32) + low.astype(F32)).astype(BF16), before[half:]]
    )
    after = jnp.concatenate(
        [after[:half], (after[half:].astype(F32) + high.astype(F32)).astype(BF16)]
    )
    one = shift(before, axis, -1)
    two = shift(after, axis, 1)
    return (own.astype(F32) + one.astype(F32) + two.astype(F32)).astype(BF16)


def expert_kernel(
    starts, picks, tiles, source, states, ranks, shares,
    gate0, up0, down0, gate1, up1, down1, out_a, out_b, rows_ref,
):
    step = pl.program_id(0)
    blocks = ranks.shape[0]
    half = out_a.shape[1]

    def mask_of(block, part):
        lane_rank = ranks[block]
        wanted = (lax.broadcasted_iota(I32, (PICK, BLOCK), 0) + part * PICK).astype(F32)
        return [jnp.where(lane_rank[e : e + 1, :] == wanted, 1.0, 0.0) for e in range(4)]

    def place(expert, block, part):
        return pl.ds(pl.multiple_of(starts[expert * blocks + block] + part * PICK, 16), PICK)

    @pl.when(step == 0)
    def _():
        def one_block(block, carry):
            held = jnp.concatenate([states[source[2 * block]], states[source[2 * block + 1]]])

            def one_part(part, carry):
                mask = jnp.concatenate(mask_of(block, part)).astype(BF16)
                got = jnp.dot(mask, held, preferred_element_type=F32).astype(BF16)
                for e in range(4):
                    rows_ref[e, place(e, block, part), :] = got[e * PICK : (e + 1) * PICK]
                return carry

            return lax.fori_loop(0, picks[block], one_part, carry)

        lax.fori_loop(0, blocks, one_block, 0)

    def feed_forward(expert, gate, up, down):
        def one_tile(tile, carry):
            at = pl.ds(pl.multiple_of(tile * BLOCK, BLOCK), BLOCK)
            held = rows_ref[expert, at, :]
            gated = jnp.dot(held, gate[0], preferred_element_type=F32)
            raised = jnp.dot(held, up[0], preferred_element_type=F32)
            hidden = (gated / (1.0 + jnp.exp(-gated)) * raised).astype(BF16)
            rows_ref[expert, at, :] = jnp.dot(
                hidden, down[0], preferred_element_type=F32
            ).astype(BF16)
            return carry

        lax.fori_loop(0, tiles[expert], one_tile, 0)

    @pl.when((step == 1) | (step == 2))
    def _():
        feed_forward(step - 1, gate0, up0, down0)

    @pl.when((step == 3) | (step == 4))
    def _():
        feed_forward(step - 1, gate1, up1, down1)

    @pl.when(step == 5)
    def _():
        def one_block(block, carry):
            share = shares[block]

            def one_part(part, total):
                masks = mask_of(block, part)
                weight = jnp.concatenate([masks[e] * share[e : e + 1, :] for e in range(4)])
                high = weight.astype(BF16)
                low = (weight - high.astype(F32)).astype(BF16)
                made = jnp.concatenate([rows_ref[e, place(e, block, part), :] for e in range(4)])
                dims = (((0,), (0,)), ((), ()))
                total = total + lax.dot_general(high, made, dims, preferred_element_type=F32)
                return total + lax.dot_general(low, made, dims, preferred_element_type=F32)

            total = lax.fori_loop(
                0, picks[block], one_part, jnp.zeros((BLOCK, out_a.shape[2]), F32)
            ).astype(BF16)
            for j in range(2):
                at = 2 * block + j
                base = j * 2 * half
                out_a[lax.rem(at, 4) * 4 + lax.div(at, 4)] = total[base : base + half]
                out_b[at] = total[base + half : base + 2 * half]
            return carry

        lax.fori_loop(0, blocks, one_block, 0)


def run_experts(starts, picks, tiles, source, states, ranks, shares, own, other):
    features = states.shape[2]
    hidden = own[0].shape[2]
    blocks = ranks.shape[0]
    slots, tokens = states.shape[0], states.shape[1]
    half = tokens // 2
    whole3 = lambda i, *_: (0, 0, 0)
    first = lambda i, *_: (jnp.clip(i - 1, 0, 1), 0, 0)
    second = lambda i, *_: (jnp.clip(i - 3, 0, 1), 0, 0)
    weights = lambda at: [
        pl.BlockSpec((1, features, hidden), at),
        pl.BlockSpec((1, features, hidden), at),
        pl.BlockSpec((1, hidden, features), at),
    ]
    shape = jax.ShapeDtypeStruct((slots, half, features), BF16)
    return pl.pallas_call(
        expert_kernel,
        grid_spec=pltpu.PrefetchScalarGridSpec(
            num_scalar_prefetch=4,
            grid=(6,),
            in_specs=[
                pl.BlockSpec(states.shape, whole3),
                pl.BlockSpec(ranks.shape, whole3),
                pl.BlockSpec(shares.shape, whole3),
                *weights(first),
                *weights(second),
            ],
            out_specs=[pl.BlockSpec(shape.shape, whole3)] * 2,
            scratch_shapes=[pltpu.VMEM((4, slots * tokens + BLOCK, features), BF16)],
        ),
        out_shape=[shape, shape],
        compiler_params=pltpu.CompilerParams(vmem_limit_bytes=60 * 1024 * 1024),
        cost_estimate=pl.CostEstimate(
            flops=8 * slots * tokens * features * hidden,
            bytes_accessed=30_000_000,
            transcendentals=0,
        ),
    )(starts, picks, tiles, source, states, ranks, shares, *own, *other)


def body(policy_states, row_lengths, send_order, expert_ids, gate_codes, w_gate, w_up, w_down):
    features = policy_states.shape[3]
    maxlen = policy_states.shape[2]
    top = expert_ids.shape[-1]
    x, y, core = (lax.axis_index(name) for name in PLANE)
    column = (x * 4 + y) * 2 + core
    device = lax.axis_index("dp") * 32 + column
    swap = [(0, 1), (1, 0)]
    other = [lax.ppermute(w, "core", swap) for w in (w_gate, w_up, w_down)]

    packed = jnp.concatenate([row_lengths, send_order])
    spread = lax.all_to_all(
        jnp.broadcast_to(packed[None], (32, 16)), PLANE, 0, 0, tiled=True
    )
    lengths = spread[:, :8].T.reshape(256)
    held_by = (spread[:, 8:].T * 32 + jnp.arange(32, dtype=I32)[None, :]).reshape(256)
    every = jnp.arange(256, dtype=I32)
    offsets = jnp.sum(jnp.where(every[None, :] < every[:, None], lengths[None, :], 0), axis=1)
    is_holder = held_by[:, None] == every[None, :]
    judge_offsets = jnp.sum(jnp.where(is_holder, offsets[None, :], 0), axis=1)
    judge_lengths = jnp.sum(jnp.where(is_holder, lengths[None, :], 0), axis=1)
    at_me = every == device
    mine = jnp.sum(jnp.where(at_me, offsets, 0))
    judged_at = jnp.sum(jnp.where(at_me, judge_offsets, 0))
    judged_len = jnp.sum(jnp.where(at_me, judge_lengths, 0))

    pairs = jnp.arange(2 * 256, dtype=I32)
    peer, turn = pairs // 2, pairs % 2
    positions = jnp.arange(maxlen, dtype=I32)
    sent = lambda offset: (peer - offset) % 256 + 256 * turn
    rows = pick(one_hot(sent(mine), positions), policy_states.reshape(maxlen, features))
    names = jnp.concatenate(
        [
            expert_ids.reshape(maxlen, top).astype(BF16),
            gate_codes.reshape(maxlen, top).astype(BF16),
            jnp.zeros((maxlen, 128 - 2 * top), BF16),
        ],
        axis=1,
    )
    names = pick(one_hot(sent(judged_at), positions), names)
    outbound = jnp.concatenate([rows, names], axis=1).reshape(256, 2, features + 128)
    inbound = lax.all_to_all(outbound, ALL, 0, 0, tiled=True).reshape(512, features + 128)

    def slots_of(offset, length):
        offset, length = jnp.repeat(offset, 2), jnp.repeat(length, 2)
        position = (device - offset) % 256 + 256 * turn
        return jnp.where(position < length, (offset + position) // 256, -1)

    to_slot = one_hot(every, slots_of(offsets, lengths))
    judge_slot = one_hot(every, slots_of(judge_offsets, judge_lengths))
    states = pick(to_slot, inbound[:, :features])
    named = lax.dot_general(
        inbound[:, features : features + 16], judge_slot, (((0,), (1,)), ((), ())),
        preferred_element_type=F32,
    ).astype(BF16)

    all_named = lax.all_gather(named, ("x", "y"), axis=0).reshape(4, 4, 16, 256)
    all_named = lax.dynamic_slice_in_dim(jnp.concatenate([all_named, all_named], 0), x, 4, 0)
    all_named = lax.dynamic_slice_in_dim(jnp.concatenate([all_named, all_named], 1), y, 4, 1)
    near = jnp.arange(16, dtype=I32)
    source = (x + near // 4) % 4 * 4 + (y + near % 4) % 4
    experts = jnp.stack([2 * column, 2 * column + 1, 2 * (column ^ 1), 2 * (column ^ 1) + 1])
    below = (jnp.arange(BLOCK)[:, None] < jnp.arange(BLOCK)[None, :]).astype(BF16)
    size = 256 // CHUNKS
    blocks = 16 * size // BLOCK
    finished = []
    for chunk in range(CHUNKS):
        gathered = lax.all_gather(
            states[chunk * size : (chunk + 1) * size], ("x", "y"), axis=0
        )
        named_here = all_named[..., chunk * size : (chunk + 1) * size]
        named_here = named_here.transpose(2, 0, 1, 3).reshape(16, 16 * size)
        codes = named_here[top : 2 * top].astype(F32)
        share = codes / jnp.sum(codes, axis=0, keepdims=True)
        hit = named_here[None, :top].astype(I32) == experts[:, None, None]
        mask = jnp.any(hit, axis=1)
        shares = jnp.sum(jnp.where(hit, share[None], 0.0), axis=1)
        mask = mask.reshape(4, blocks, BLOCK)
        rank = jnp.dot(
            mask.reshape(4 * blocks, BLOCK).astype(BF16), below, preferred_element_type=F32
        ).reshape(4, blocks, BLOCK)
        ranks = jnp.where(mask, rank, -1.0).transpose(1, 0, 2)
        shares = shares.reshape(4, blocks, BLOCK).transpose(1, 0, 2)
        count = jnp.sum(mask.astype(I32), axis=2)
        taken = (count + 15) // 16 * 16
        earlier = jnp.arange(blocks)[None, :] < jnp.arange(blocks)[:, None]
        starts = jnp.sum(jnp.where(earlier[None], taken[:, None, :], 0), axis=2)
        tiles = (jnp.sum(taken, axis=1) + BLOCK - 1) // BLOCK
        picks = jnp.max((count + PICK - 1) // PICK, axis=0)
        out_a, out_b = run_experts(
            starts.reshape(-1), picks, tiles, source, gathered, ranks, shares,
            (w_gate, w_up, w_down), other,
        )
        flat = 8 * size
        finished.append(ring_sum(ring_sum(out_a.reshape(flat, features), "y"), "x"))
        finished.append(ring_sum(ring_sum(out_b.reshape(flat, features), "x"), "y"))

    made = jnp.concatenate(finished)
    back = lax.dot_general(
        judge_slot, made, (((0,), (0,)), ((), ())), preferred_element_type=F32
    ).astype(BF16)
    back = lax.all_to_all(back.reshape(256, 2, features), ALL, 0, 0, tiled=True)
    found = jnp.where(
        positions < judged_len, (positions + judged_at) % 256 * 2 + positions // 256, -1
    )
    result = pick(one_hot(found, pairs), back.reshape(512, features))
    return result.reshape(1, maxlen, features)


def solution(mesh):
    fine = Mesh(mesh.devices.reshape(8, 4, 4, 2), ALL)
    in_specs = (
        P(PLANE, "dp", None, None),
        P(PLANE),
        P(PLANE),
        P("dp", PLANE, None, None),
        P("dp", PLANE, None, None),
        P(PLANE, None, None),
        P(PLANE, None, None),
        P(PLANE, None, None),
    )
    return jax.shard_map(
        body, mesh=fine, in_specs=in_specs, out_specs=P(ALL, None, None), check_vma=False
    )
```

```python
import functools

import jax
import jax.numpy as jnp
from jax import lax
from jax.experimental import pallas as pl
from jax.experimental.pallas import tpu as pltpu
from jax.sharding import Mesh, PartitionSpec as P

F32 = jnp.float32
BF16 = jnp.bfloat16
I32 = jnp.int32
ALL = ("dp", "x", "y", "core")
PLANE = ("x", "y", "core")
CHUNKS = 2
BLOCK = 256
PICK = 64


def one_hot(rows, columns):
    return (rows[:, None] == columns[None, :]).astype(BF16)


def pick(matrix, values):
    return jnp.dot(matrix, values, preferred_element_type=F32).astype(BF16)


def shift(value, axis, by):
    size = lax.axis_size(axis)
    return lax.ppermute(value, axis, [(i, (i + by) % size) for i in range(size)])


def ring_sum(value, axis):
    rows = value.shape[0] // 4
    half = rows // 2
    own, after, across, before = (value[i * rows : (i + 1) * rows] for i in range(4))
    low = shift(across[:half], axis, -1)
    high = shift(across[half:], axis, 1)
    before = jnp.concatenate(
        [(before[:half].astype(F32) + low.astype(F32)).astype(BF16), before[half:]]
    )
    after = jnp.concatenate(
        [after[:half], (after[half:].astype(F32) + high.astype(F32)).astype(BF16)]
    )
    one = shift(before, axis, -1)
    two = shift(after, axis, 1)
    return (own.astype(F32) + one.astype(F32) + two.astype(F32)).astype(BF16)


def ring_gather(value, axis):
    half = value.shape[0] // 2
    after = shift(value, axis, -1)
    before = shift(value, axis, 1)
    low = shift(after[:half], axis, -1)
    high = shift(before[half:], axis, 1)
    return jnp.concatenate([value, after, low, high, before])


def near_names(value, axis):
    return jnp.stack([value, *(shift(value, axis, -by) for by in (1, 2, 3))])


def expert_kernel(
    starts, picks, tiles, source, target, states, ranks, shares,
    gate0, up0, down0, gate1, up1, down1, out,
    rows_ref, gate_ref, up_ref, down_ref, in_ref, out_ref, sum_ref, in_sems, out_sems, w_sems,
):
    blocks = ranks.shape[0]
    size = in_ref.shape[1] // 2

    def load(block, half):
        slot = lax.rem(block, 2)
        return pltpu.make_async_copy(
            states.at[source[2 * block + half], pl.ds(0, size)],
            in_ref.at[slot, pl.ds(half * size, size)],
            in_sems.at[slot, half],
        )

    def save(block, half):
        slot = lax.rem(block, 2)
        return pltpu.make_async_copy(
            out_ref.at[slot, pl.ds(half * size, size)],
            out.at[target[2 * block + half]],
            out_sems.at[slot, half],
        )

    def weight_copies(expert):
        gate, up, down = ((gate0, up0, down0), (gate1, up1, down1))[expert // 2]
        return [
            pltpu.make_async_copy(w.at[expert % 2], ref.at[expert], w_sems.at[expert, i])
            for i, (w, ref) in enumerate(((gate, gate_ref), (up, up_ref), (down, down_ref)))
        ]

    def mask_of(block, part):
        lane_rank = ranks[block]
        wanted = (lax.broadcasted_iota(I32, (PICK, BLOCK), 0) + part * PICK).astype(F32)
        return [jnp.where(lane_rank[e : e + 1, :] == wanted, 1.0, 0.0) for e in range(4)]

    def place(expert, block, part):
        return pl.ds(pl.multiple_of(starts[expert * blocks + block] + part * PICK, 16), PICK)

    for half in range(2):
        load(0, half).start()
    for expert in range(4):
        for copy in weight_copies(expert):
            copy.start()

    def pick_block(block, carry):
        @pl.when(block + 1 < blocks)
        def _():
            for half in range(2):
                load(block + 1, half).start()

        for half in range(2):
            load(block, half).wait()
        slot = lax.rem(block, 2)

        def one_part(part, carry):
            mask = jnp.concatenate(mask_of(block, part)).astype(BF16)
            got = jnp.dot(mask, in_ref[slot], preferred_element_type=F32).astype(BF16)
            for e in range(4):
                rows_ref[e, place(e, block, part), :] = got[e * PICK : (e + 1) * PICK]
            return carry

        one_part(0, 0)
        return lax.fori_loop(1, picks[block], one_part, carry)

    lax.fori_loop(0, blocks, pick_block, 0)

    for expert in range(4):
        for copy in weight_copies(expert):
            copy.wait()

        def one_tile(tile, carry, expert=expert):
            at = pl.ds(pl.multiple_of(tile * BLOCK, BLOCK), BLOCK)
            held = rows_ref[expert, at, :]
            turned = (((1,), (1,)), ((), ()))
            gated = lax.dot_general(held, gate_ref[expert], turned, preferred_element_type=F32)
            raised = lax.dot_general(held, up_ref[expert], turned, preferred_element_type=F32)
            hidden = (gated / (1.0 + jnp.exp(-gated)) * raised).astype(BF16)
            rows_ref[expert, at, :] = jnp.dot(
                hidden, down_ref[expert], preferred_element_type=F32
            ).astype(BF16)
            return carry

        lax.fori_loop(0, tiles[expert], one_tile, 0)

    def sum_block(block, carry):
        share = shares[block]
        slot = lax.rem(block, 2)

        def one_part(part):
            masks = mask_of(block, part)
            weight = jnp.concatenate([masks[e] * share[e : e + 1, :] for e in range(4)])
            high = weight.astype(BF16)
            low = (weight - high.astype(F32)).astype(BF16)
            made = jnp.concatenate([rows_ref[e, place(e, block, part), :] for e in range(4)])
            dims = (((0,), (0,)), ((), ()))
            return lax.dot_general(
                high, made, dims, preferred_element_type=F32
            ) + lax.dot_general(low, made, dims, preferred_element_type=F32)

        @pl.when(block >= 2)
        def _():
            for half in range(2):
                save(block - 2, half).wait()

        out_ref[slot] = one_part(0).astype(BF16)

        @pl.when(picks[block] > 1)
        def _():
            sum_ref[...] = one_part(0)

            def add_part(part, carry):
                sum_ref[...] += one_part(part)
                return carry

            lax.fori_loop(1, picks[block], add_part, 0)
            out_ref[slot] = sum_ref[...].astype(BF16)

        for half in range(2):
            save(block, half).start()
        return carry

    lax.fori_loop(0, blocks, sum_block, 0)
    for block in (blocks - 2, blocks - 1):
        for half in range(2):
            save(block, half).wait()


def run_experts(starts, picks, tiles, source, target, states, ranks, shares, own, other):
    features = states.shape[2]
    hidden = own[0].shape[1]
    slots = states.shape[0]
    size = BLOCK // 2
    anywhere = pl.BlockSpec(memory_space=pl.ANY)
    whole = pl.BlockSpec(ranks.shape, lambda *_: (0, 0, 0))
    return pl.pallas_call(
        expert_kernel,
        grid_spec=pltpu.PrefetchScalarGridSpec(
            num_scalar_prefetch=5,
            grid=(1,),
            in_specs=[anywhere, whole, whole] + [anywhere] * 6,
            out_specs=anywhere,
            scratch_shapes=[
                pltpu.VMEM((4, slots * size + BLOCK, features), BF16),
                pltpu.VMEM((4, hidden, features), BF16),
                pltpu.VMEM((4, hidden, features), BF16),
                pltpu.VMEM((4, hidden, features), BF16),
                pltpu.VMEM((2, BLOCK, features), BF16),
                pltpu.VMEM((2, BLOCK, features), BF16),
                pltpu.VMEM((BLOCK, features), F32),
                pltpu.SemaphoreType.DMA((2, 2)),
                pltpu.SemaphoreType.DMA((2, 2)),
                pltpu.SemaphoreType.DMA((4, 3)),
            ],
        ),
        out_shape=jax.ShapeDtypeStruct((slots, size, features), BF16),
        compiler_params=pltpu.CompilerParams(vmem_limit_bytes=52 * 1024 * 1024),
        cost_estimate=pl.CostEstimate(
            flops=8 * slots * size * features * hidden,
            bytes_accessed=26_000_000,
            transcendentals=0,
        ),
    )(starts, picks, tiles, source, target, states, ranks, shares, *own, *other)


def body(policy_states, row_lengths, send_order, expert_ids, gate_codes, w_gate, w_up, w_down):
    features = policy_states.shape[3]
    maxlen = policy_states.shape[2]
    top = expert_ids.shape[-1]
    x, y, core = (lax.axis_index(name) for name in PLANE)
    column = (x * 4 + y) * 2 + core
    device = lax.axis_index("dp") * 32 + column
    swap = [(0, 1), (1, 0)]
    own = [jnp.swapaxes(w_gate, 1, 2), jnp.swapaxes(w_up, 1, 2), w_down]
    other = [lax.ppermute(w, "core", swap) for w in own]

    packed = jnp.concatenate([row_lengths, send_order])
    spread = lax.all_to_all(
        jnp.broadcast_to(packed[None], (32, 16)), PLANE, 0, 0, tiled=True
    )
    lengths = spread[:, :8].T.reshape(256)
    held_by = (spread[:, 8:].T * 32 + jnp.arange(32, dtype=I32)[None, :]).reshape(256)
    every = jnp.arange(256, dtype=I32)
    offsets = jnp.sum(jnp.where(every[None, :] < every[:, None], lengths[None, :], 0), axis=1)
    is_holder = held_by[:, None] == every[None, :]
    judge_offsets = jnp.sum(jnp.where(is_holder, offsets[None, :], 0), axis=1)
    judge_lengths = jnp.sum(jnp.where(is_holder, lengths[None, :], 0), axis=1)
    at_me = every == device
    mine = jnp.sum(jnp.where(at_me, offsets, 0))
    judged_at = jnp.sum(jnp.where(at_me, judge_offsets, 0))
    judged_len = jnp.sum(jnp.where(at_me, judge_lengths, 0))

    pairs = jnp.arange(2 * 256, dtype=I32)
    peer, turn = pairs // 2, pairs % 2
    positions = jnp.arange(maxlen, dtype=I32)
    sent = lambda offset: (peer - offset) % 256 + 256 * turn
    rows = pick(one_hot(sent(mine), positions), policy_states.reshape(maxlen, features))
    names = jnp.concatenate(
        [
            expert_ids.reshape(maxlen, top).astype(BF16),
            gate_codes.reshape(maxlen, top).astype(BF16),
            jnp.zeros((maxlen, 128 - 2 * top), BF16),
        ],
        axis=1,
    )
    names = pick(one_hot(sent(judged_at), positions), names)
    outbound = jnp.concatenate([rows, names], axis=1).reshape(256, 2, features + 128)
    inbound = lax.all_to_all(outbound, ALL, 0, 0, tiled=True).reshape(512, features + 128)

    def slots_of(offset, length):
        offset, length = jnp.repeat(offset, 2), jnp.repeat(length, 2)
        position = (device - offset) % 256 + 256 * turn
        return jnp.where(position < length, (offset + position) // 256, -1)

    to_slot = one_hot(every, slots_of(offsets, lengths))
    judge_slot = one_hot(every, slots_of(judge_offsets, judge_lengths))
    states = pick(to_slot, inbound[:, :features])
    named = lax.dot_general(
        inbound[:, features : features + 16], judge_slot, (((0,), (1,)), ((), ())),
        preferred_element_type=F32,
    ).astype(BF16)

    all_named = near_names(near_names(named, "y"), "x")
    near = jnp.arange(16, dtype=I32)
    source = (x + near // 4) % 4 * 4 + (y + near % 4) % 4
    experts = jnp.stack([2 * column, 2 * column + 1, 2 * (column ^ 1), 2 * (column ^ 1) + 1])
    below = (jnp.arange(BLOCK)[:, None] < jnp.arange(BLOCK)[None, :]).astype(BF16)
    size = 256 // CHUNKS
    blocks = 16 * size // BLOCK
    gathered = [
        lax.all_gather(states[:size], ("x", "y"), axis=0),
        ring_gather(ring_gather(states[size:], "y"), "x").reshape(16, size, features),
    ]
    sources = [source, near]
    targets = [near % 4 * 4 + near // 4, near]
    finished = []
    for chunk in range(CHUNKS):
        named_here = all_named[..., chunk * size : (chunk + 1) * size]
        named_here = named_here.transpose(2, 0, 1, 3).reshape(16, 16 * size)
        codes = named_here[top : 2 * top].astype(F32)
        share = codes / jnp.sum(codes, axis=0, keepdims=True)
        hit = named_here[None, :top].astype(I32) == experts[:, None, None]
        mask = jnp.any(hit, axis=1)
        shares = jnp.sum(jnp.where(hit, share[None], 0.0), axis=1)
        mask = mask.reshape(4, blocks, BLOCK)
        rank = jnp.dot(
            mask.reshape(4 * blocks, BLOCK).astype(BF16), below, preferred_element_type=F32
        ).reshape(4, blocks, BLOCK)
        ranks = jnp.where(mask, rank, -1.0).transpose(1, 0, 2)
        shares = shares.reshape(4, blocks, BLOCK).transpose(1, 0, 2)
        count = jnp.sum(mask.astype(I32), axis=2)
        taken = (count + 15) // 16 * 16
        earlier = jnp.arange(blocks)[None, :] < jnp.arange(blocks)[:, None]
        starts = jnp.sum(jnp.where(earlier[None], taken[:, None, :], 0), axis=2)
        tiles = (jnp.sum(taken, axis=1) + BLOCK - 1) // BLOCK
        picks = jnp.max((count + PICK - 1) // PICK, axis=0)
        made = run_experts(
            starts.reshape(-1), picks, tiles, sources[chunk], targets[chunk], gathered[chunk],
            ranks, shares, own, other,
        ).reshape(16 * size, features)
        first, second = (("y", "x"), ("x", "y"))[chunk]
        finished.append(ring_sum(ring_sum(made, first), second))

    made = jnp.concatenate(finished)
    back = lax.dot_general(
        judge_slot, made, (((0,), (0,)), ((), ())), preferred_element_type=F32
    ).astype(BF16)
    back = lax.all_to_all(back.reshape(256, 2, features), ALL, 0, 0, tiled=True)
    found = jnp.where(
        positions < judged_len, (positions + judged_at) % 256 * 2 + positions // 256, -1
    )
    result = pick(one_hot(found, pairs), back.reshape(512, features))
    return result.reshape(1, maxlen, features)


def solution(mesh):
    fine = Mesh(mesh.devices.reshape(8, 4, 4, 2), ALL)
    in_specs = (
        P(PLANE, "dp", None, None),
        P(PLANE),
        P(PLANE),
        P("dp", PLANE, None, None),
        P("dp", PLANE, None, None),
        P(PLANE, None, None),
        P(PLANE, None, None),
        P(PLANE, None, None),
    )
    return jax.shard_map(
        body, mesh=fine, in_specs=in_specs, out_specs=P(ALL, None, None), check_vma=False
    )
```

```python
import functools

import jax
import jax.numpy as jnp
from jax import lax
from jax.experimental import pallas as pl
from jax.experimental.pallas import tpu as pltpu
from jax.sharding import Mesh, PartitionSpec as P

F32 = jnp.float32
BF16 = jnp.bfloat16
I32 = jnp.int32
ALL = ("dp", "x", "y", "core")
PLANE = ("x", "y", "core")
CHUNKS = 2
BLOCK = 256
PICK = 64


def one_hot(rows, columns):
    return (rows[:, None] == columns[None, :]).astype(BF16)


def pick(matrix, values):
    return jnp.dot(matrix, values, preferred_element_type=F32).astype(BF16)


def shift(value, axis, by):
    size = lax.axis_size(axis)
    return lax.ppermute(value, axis, [(i, (i + by) % size) for i in range(size)])


def together(values):
    return list(lax.optimization_barrier(tuple(values)))


def add(*values):
    return sum(value.astype(F32) for value in values).astype(BF16)


def gather_plane(one, two):
    steps = (-1, -2, 1)
    lines = together([shift(one, "x", by) for by in steps] + [shift(two, "y", by) for by in steps])
    one = jnp.concatenate([one, *lines[:3]])
    two = jnp.concatenate([two, *lines[3:]])
    one, two = together([one, two])
    near = together([shift(v, axis, by) for v, axis in ((one, "y"), (two, "x")) for by in (-1, 1)])
    half = one.shape[0] // 2
    far = together(
        [
            shift(near[0][:half], "y", -1),
            shift(near[1][half:], "y", 1),
            shift(near[2][:half], "x", -1),
            shift(near[3][half:], "x", 1),
        ]
    )
    return (one, near[0], far[0], far[1], near[1]), (two, near[2], far[2], far[3], near[3])


def send_across(pieces, axis):
    return [shift(pieces[2], axis, -1), shift(pieces[3], axis, 1)]


def sum_line(pieces, across, axis):
    own, after, _, _, before = pieces
    half = own.shape[0] // 2
    low, high = across
    before = add(before, jnp.pad(low, ((0, half), (0, 0))))
    after = add(after, jnp.pad(high, ((half, 0), (0, 0))))
    return add(own, *together([shift(before, axis, -1), shift(after, axis, 1)]))


def sum_last(value, axis):
    value = value.reshape(4, -1, value.shape[1])
    blocks = together([value[i] for i in range(4)])
    found = together([shift(blocks[i], axis, by) for i, by in ((1, 1), (2, 2), (3, -1))])
    return add(blocks[0], *found)


def from_here(value, axis, dim):
    twice = jnp.concatenate([value, value], dim)
    return lax.dynamic_slice_in_dim(twice, lax.axis_index(axis), value.shape[dim], dim)


def expert_kernel(starts, picks, tiles, *refs):
    pieces, (ranks, shares), weights, outs, scratch = (
        refs[:5], refs[5:7], refs[7:13], refs[13:18], refs[18:],
    )
    gate0, up0, down0, gate1, up1, down1 = weights
    rows_ref, gate_ref, up_ref, down_ref, in_ref, out_ref, sum_ref = scratch[:7]
    in_sems, out_sems, w_sems = scratch[7:]
    blocks = ranks.shape[0]

    def part_of(refs, block):
        piece, at = ((0, 0), (0, 1), (1, 0), (1, 1), (2, 0), (3, 0), (4, 0), (4, 1))[block]
        return refs[piece].at[pl.ds(at * BLOCK, BLOCK)]

    def load(block):
        return pltpu.make_async_copy(part_of(pieces, block), in_ref.at[block], in_sems.at[block])

    def save(block):
        return pltpu.make_async_copy(out_ref.at[block], part_of(outs, block), out_sems.at[block])

    def when_at(block, action):
        for each in range(blocks):
            pl.when(block == each)(functools.partial(action, each))

    def weight_copies(expert):
        gate, up, down = ((gate0, up0, down0), (gate1, up1, down1))[expert // 2]
        return [
            pltpu.make_async_copy(w.at[expert % 2], ref.at[expert], w_sems.at[expert, i])
            for i, (w, ref) in enumerate(((gate, gate_ref), (up, up_ref), (down, down_ref)))
        ]

    def mask_of(block, part):
        lane_rank = ranks[block]
        wanted = (lax.broadcasted_iota(I32, (PICK, BLOCK), 0) + part * PICK).astype(F32)
        return [jnp.where(lane_rank[e : e + 1, :] == wanted, 1.0, 0.0) for e in range(4)]

    def place(expert, block, part):
        return pl.ds(pl.multiple_of(starts[expert * blocks + block] + part * PICK, 16), PICK)

    for block in range(blocks):
        load(block).start()
    for expert in range(4):
        for copy in weight_copies(expert):
            copy.start()

    def pick_block(block, carry):
        when_at(block, lambda each: load(each).wait())

        def one_part(part, carry):
            mask = jnp.concatenate(mask_of(block, part)).astype(BF16)
            got = jnp.dot(mask, in_ref[block], preferred_element_type=F32).astype(BF16)
            for e in range(4):
                rows_ref[e, place(e, block, part), :] = got[e * PICK : (e + 1) * PICK]
            return carry

        one_part(0, 0)
        return lax.fori_loop(1, picks[block], one_part, carry)

    lax.fori_loop(0, blocks, pick_block, 0)

    for expert in range(4):
        for copy in weight_copies(expert):
            copy.wait()

        def one_tile(tile, carry, expert=expert):
            at = pl.ds(pl.multiple_of(tile * BLOCK, BLOCK), BLOCK)
            held = rows_ref[expert, at, :]
            turned = (((1,), (1,)), ((), ()))
            gated = lax.dot_general(held, gate_ref[expert], turned, preferred_element_type=F32)
            raised = lax.dot_general(held, up_ref[expert], turned, preferred_element_type=F32)
            hidden = (gated / (1.0 + jnp.exp(-gated)) * raised).astype(BF16)
            rows_ref[expert, at, :] = jnp.dot(
                hidden, down_ref[expert], preferred_element_type=F32
            ).astype(BF16)
            return carry

        lax.fori_loop(0, tiles[expert], one_tile, 0)

    def sum_block(block, carry):
        share = shares[block]

        def one_part(part):
            masks = mask_of(block, part)
            weight = jnp.concatenate([masks[e] * share[e : e + 1, :] for e in range(4)])
            high = weight.astype(BF16)
            low = (weight - high.astype(F32)).astype(BF16)
            made = jnp.concatenate([rows_ref[e, place(e, block, part), :] for e in range(4)])
            dims = (((0,), (0,)), ((), ()))
            return lax.dot_general(
                high, made, dims, preferred_element_type=F32
            ) + lax.dot_general(low, made, dims, preferred_element_type=F32)

        out_ref[block] = one_part(0).astype(BF16)

        @pl.when(picks[block] > 1)
        def _():
            sum_ref[...] = one_part(0)

            def add_part(part, carry):
                sum_ref[...] += one_part(part)
                return carry

            lax.fori_loop(1, picks[block], add_part, 0)
            out_ref[block] = sum_ref[...].astype(BF16)

        when_at(block, lambda each: save(each).start())
        return carry

    lax.fori_loop(0, blocks, sum_block, 0)
    for block in range(blocks):
        save(block).wait()


def run_experts(starts, picks, tiles, pieces, ranks, shares, own, other):
    features = pieces[0].shape[1]
    hidden = own[0].shape[1]
    blocks = ranks.shape[0]
    tokens = blocks * BLOCK
    anywhere = pl.BlockSpec(memory_space=pl.ANY)
    whole = pl.BlockSpec(ranks.shape, lambda *_: (0, 0, 0))
    return pl.pallas_call(
        expert_kernel,
        grid_spec=pltpu.PrefetchScalarGridSpec(
            num_scalar_prefetch=3,
            grid=(1,),
            in_specs=[anywhere] * 5 + [whole] * 2 + [anywhere] * 6,
            out_specs=[anywhere] * 5,
            scratch_shapes=[
                pltpu.VMEM((4, tokens + BLOCK, features), BF16),
                pltpu.VMEM((4, hidden, features), BF16),
                pltpu.VMEM((4, hidden, features), BF16),
                pltpu.VMEM((4, hidden, features), BF16),
                pltpu.VMEM((blocks, BLOCK, features), BF16),
                pltpu.VMEM((blocks, BLOCK, features), BF16),
                pltpu.VMEM((BLOCK, features), F32),
                pltpu.SemaphoreType.DMA((blocks,)),
                pltpu.SemaphoreType.DMA((blocks,)),
                pltpu.SemaphoreType.DMA((4, 3)),
            ],
        ),
        out_shape=[jax.ShapeDtypeStruct(piece.shape, BF16) for piece in pieces],
        compiler_params=pltpu.CompilerParams(vmem_limit_bytes=56 * 1024 * 1024),
        cost_estimate=pl.CostEstimate(
            flops=8 * tokens * features * hidden, bytes_accessed=26_000_000, transcendentals=0
        ),
    )(starts, picks, tiles, *pieces, ranks, shares, *own, *other)


def body(policy_states, row_lengths, send_order, expert_ids, gate_codes, w_gate, w_up, w_down):
    features = policy_states.shape[3]
    maxlen = policy_states.shape[2]
    top = expert_ids.shape[-1]
    x, y, core = (lax.axis_index(name) for name in PLANE)
    column = (x * 4 + y) * 2 + core
    device = lax.axis_index("dp") * 32 + column
    swap = [(0, 1), (1, 0)]
    own = [jnp.swapaxes(w_gate, 1, 2), jnp.swapaxes(w_up, 1, 2), w_down]
    other = [lax.ppermute(w, "core", swap) for w in own]

    packed = jnp.concatenate([row_lengths, send_order])
    spread = lax.all_to_all(
        jnp.broadcast_to(packed[None], (32, 16)), PLANE, 0, 0, tiled=True
    )
    lengths = spread[:, :8].T.reshape(256)
    held_by = (spread[:, 8:].T * 32 + jnp.arange(32, dtype=I32)[None, :]).reshape(256)
    every = jnp.arange(256, dtype=I32)
    offsets = jnp.sum(jnp.where(every[None, :] < every[:, None], lengths[None, :], 0), axis=1)
    is_holder = held_by[:, None] == every[None, :]
    judge_offsets = jnp.sum(jnp.where(is_holder, offsets[None, :], 0), axis=1)
    judge_lengths = jnp.sum(jnp.where(is_holder, lengths[None, :], 0), axis=1)
    at_me = every == device
    mine = jnp.sum(jnp.where(at_me, offsets, 0))
    judged_at = jnp.sum(jnp.where(at_me, judge_offsets, 0))
    judged_len = jnp.sum(jnp.where(at_me, judge_lengths, 0))

    pairs = jnp.arange(2 * 256, dtype=I32)
    peer, turn = pairs // 2, pairs % 2
    positions = jnp.arange(maxlen, dtype=I32)
    sent = lambda offset: (peer - offset) % 256 + 256 * turn
    rows = pick(one_hot(sent(mine), positions), policy_states.reshape(maxlen, features))
    names = jnp.concatenate(
        [
            expert_ids.reshape(maxlen, top).astype(BF16),
            gate_codes.reshape(maxlen, top).astype(BF16),
            jnp.zeros((maxlen, 128 - 2 * top), BF16),
        ],
        axis=1,
    )
    names = pick(one_hot(sent(judged_at), positions), names)
    outbound = jnp.concatenate([rows, names], axis=1).reshape(256, 2, features + 128)
    inbound = lax.all_to_all(outbound, ALL, 0, 0, tiled=True)
    inbound, *other = together([inbound, *other])
    inbound = inbound.reshape(512, features + 128)

    def slots_of(offset, length):
        offset, length = jnp.repeat(offset, 2), jnp.repeat(length, 2)
        position = (device - offset) % 256 + 256 * turn
        return jnp.where(position < length, (offset + position) // 256, -1)

    to_slot = one_hot(every, slots_of(offsets, lengths))
    judge_slot = one_hot(every, slots_of(judge_offsets, judge_lengths))
    states = pick(to_slot, inbound[:, :features])
    named = lax.dot_general(
        inbound[:, features : features + 16], judge_slot, (((0,), (1,)), ((), ())),
        preferred_element_type=F32,
    ).astype(BF16)

    all_named = lax.all_to_all(
        jnp.broadcast_to(named[None], (16, *named.shape)), ("x", "y"), 0, 0, tiled=True
    ).reshape(4, 4, *named.shape)
    all_named = from_here(from_here(all_named, "x", 0), "y", 1)
    experts = jnp.stack([2 * column, 2 * column + 1, 2 * (column ^ 1), 2 * (column ^ 1) + 1])
    below = (jnp.arange(BLOCK)[:, None] < jnp.arange(BLOCK)[None, :]).astype(BF16)
    size = 256 // CHUNKS
    blocks = 16 * size // BLOCK
    gathered = gather_plane(states[:size], states[size:])
    made, across = [], []
    for chunk in range(CHUNKS):
        named_here = all_named[..., chunk * size : (chunk + 1) * size]
        named_here = named_here.transpose(((2, 1, 0, 3), (2, 0, 1, 3))[chunk]).reshape(16, 16 * size)
        codes = named_here[top : 2 * top].astype(F32)
        share = codes / jnp.sum(codes, axis=0, keepdims=True)
        hit = named_here[None, :top].astype(I32) == experts[:, None, None]
        mask = jnp.any(hit, axis=1)
        shares = jnp.sum(jnp.where(hit, share[None], 0.0), axis=1)
        mask = mask.reshape(4, blocks, BLOCK)
        rank = jnp.dot(
            mask.reshape(4 * blocks, BLOCK).astype(BF16), below, preferred_element_type=F32
        ).reshape(4, blocks, BLOCK)
        ranks = jnp.where(mask, rank, -1.0).transpose(1, 0, 2)
        shares = shares.reshape(4, blocks, BLOCK).transpose(1, 0, 2)
        count = jnp.sum(mask.astype(I32), axis=2)
        taken = (count + 15) // 16 * 16
        earlier = jnp.arange(blocks)[None, :] < jnp.arange(blocks)[:, None]
        starts = jnp.sum(jnp.where(earlier[None], taken[:, None, :], 0), axis=2)
        tiles = (jnp.sum(taken, axis=1) + BLOCK - 1) // BLOCK
        picks = jnp.max((count + PICK - 1) // PICK, axis=0)
        made.append(
            run_experts(
                starts.reshape(-1), picks, tiles, gathered[chunk], ranks, shares, own, other
            )
        )
        across.append(send_across(made[chunk], "yx"[chunk]))
    held = together([*across[0], *made[1]])
    across[0], made[1] = held[:2], held[2:]
    finished = [
        sum_last(sum_line(made[0], across[0], "y"), "x"),
        sum_last(sum_line(made[1], across[1], "x"), "y"),
    ]

    made = jnp.concatenate(finished)
    back = lax.dot_general(
        judge_slot, made, (((0,), (0,)), ((), ())), preferred_element_type=F32
    ).astype(BF16)
    back = lax.all_to_all(back.reshape(256, 2, features), ALL, 0, 0, tiled=True)
    found = jnp.where(
        positions < judged_len, (positions + judged_at) % 256 * 2 + positions // 256, -1
    )
    result = pick(one_hot(found, pairs), back.reshape(512, features))
    return result.reshape(1, maxlen, features)


def solution(mesh):
    fine = Mesh(mesh.devices.reshape(8, 4, 4, 2), ALL)
    in_specs = (
        P(PLANE, "dp", None, None),
        P(PLANE),
        P(PLANE),
        P("dp", PLANE, None, None),
        P("dp", PLANE, None, None),
        P(PLANE, None, None),
        P(PLANE, None, None),
        P(PLANE, None, None),
    )
    return jax.shard_map(
        body, mesh=fine, in_specs=in_specs, out_specs=P(ALL, None, None), check_vma=False
    )
```

```python
import functools

import jax
import jax.numpy as jnp
from jax import lax
from jax.experimental import pallas as pl
from jax.experimental.pallas import tpu as pltpu
from jax.sharding import Mesh, PartitionSpec as P

F32 = jnp.float32
BF16 = jnp.bfloat16
I32 = jnp.int32
ALL = ("dp", "x", "y", "core")
PLANE = ("x", "y", "core")
CHUNKS = 2
BLOCK = 256
PICK = 64
TILE = 320


def one_hot(rows, columns):
    return (rows[:, None] == columns[None, :]).astype(BF16)


def pick(matrix, values):
    return jnp.dot(matrix, values, preferred_element_type=F32).astype(BF16)


def shift(value, axis, by):
    size = lax.axis_size(axis)
    return lax.ppermute(value, axis, [(i, (i + by) % size) for i in range(size)])


def together(values):
    return list(lax.optimization_barrier(tuple(values)))


def add(*values):
    return sum(value.astype(F32) for value in values).astype(BF16)


def gather_plane(one, two, named):
    steps = (-1, -2, 1)
    lines = [shift(one, "x", by) for by in steps] + [shift(two, "y", by) for by in steps]
    lines[0], named = together([lines[0], named])
    named = lax.all_to_all(
        jnp.broadcast_to(named[None], (16, *named.shape)), ("x", "y"), 0, 0, tiled=True
    ).reshape(4, 4, *named.shape)
    lines = together(lines)
    one = jnp.concatenate([one, *lines[:3]])
    two = jnp.concatenate([two, *lines[3:]])
    one, two = together([one, two])
    near = together([shift(v, axis, by) for v, axis in ((one, "y"), (two, "x")) for by in (-1, 1)])
    half = one.shape[0] // 2
    far = together(
        [
            shift(near[0][:half], "y", -1),
            shift(near[1][half:], "y", 1),
            shift(near[2][:half], "x", -1),
            shift(near[3][half:], "x", 1),
        ]
    )
    pieces = (one, near[0], far[0], far[1], near[1]), (two, near[2], far[2], far[3], near[3])
    return pieces, named


def send_across(pieces, axis):
    return [shift(pieces[2], axis, -1), shift(pieces[3], axis, 1)]


def sum_line(pieces, across, axis):
    own, after, _, _, before = pieces
    half = own.shape[0] // 2
    low, high = across
    before = add(before, jnp.pad(low, ((0, half), (0, 0))))
    after = add(after, jnp.pad(high, ((half, 0), (0, 0))))
    return add(own, *together([shift(before, axis, -1), shift(after, axis, 1)]))


def sum_last(value, axis):
    value = value.reshape(4, -1, value.shape[1])
    blocks = together([value[i] for i in range(4)])
    found = together([shift(blocks[i], axis, by) for i, by in ((1, 1), (2, 2), (3, -1))])
    return add(blocks[0], *found)


def from_here(value, axis, dim):
    twice = jnp.concatenate([value, value], dim)
    return lax.dynamic_slice_in_dim(twice, lax.axis_index(axis), value.shape[dim], dim)


def expert_kernel(starts, picks, tiles, *refs):
    pieces, (ranks, shares), weights, outs, scratch = (
        refs[:5], refs[5:7], refs[7:13], refs[13:18], refs[18:],
    )
    gate0, up0, down0, gate1, up1, down1 = weights
    rows_ref, gate_ref, up_ref, down_ref, in_ref, out_ref, sum_ref = scratch[:7]
    in_sems, out_sems, w_sems = scratch[7:]
    blocks = ranks.shape[0]

    def part_of(refs, block):
        piece, at = ((0, 0), (0, 1), (1, 0), (1, 1), (2, 0), (3, 0), (4, 0), (4, 1))[block]
        return refs[piece].at[pl.ds(at * BLOCK, BLOCK)]

    def load(block):
        return pltpu.make_async_copy(part_of(pieces, block), in_ref.at[block], in_sems.at[block])

    def save(block):
        return pltpu.make_async_copy(out_ref.at[block], part_of(outs, block), out_sems.at[block])

    def when_at(block, action):
        for each in range(blocks):
            pl.when(block == each)(functools.partial(action, each))

    def weight_copies(expert):
        gate, up, down = ((gate0, up0, down0), (gate1, up1, down1))[expert // 2]
        return [
            pltpu.make_async_copy(w.at[expert % 2], ref.at[expert], w_sems.at[expert, i])
            for i, (w, ref) in enumerate(((gate, gate_ref), (up, up_ref), (down, down_ref)))
        ]

    def mask_of(block, part):
        lane_rank = ranks[block]
        wanted = (lax.broadcasted_iota(I32, (PICK, BLOCK), 0) + part * PICK).astype(F32)
        return [jnp.where(lane_rank[e : e + 1, :] == wanted, 1.0, 0.0) for e in range(4)]

    def place(expert, block, part):
        return pl.ds(pl.multiple_of(starts[expert * blocks + block] + part * PICK, 16), PICK)

    for block in range(blocks):
        load(block).start()

    def fetch(expert):
        for copy in weight_copies(expert):
            copy.start()

    def pick_block(block, carry):
        when_at(block, lambda each: load(each).wait())
        pl.when(block == 0)(functools.partial(fetch, 0))
        pl.when(block == blocks // 2)(functools.partial(fetch, 1))

        def one_part(part, carry):
            mask = jnp.concatenate(mask_of(block, part)).astype(BF16)
            got = jnp.dot(mask, in_ref[block], preferred_element_type=F32).astype(BF16)
            for e in range(4):
                rows_ref[e, place(e, block, part), :] = got[e * PICK : (e + 1) * PICK]
            return carry

        one_part(0, 0)
        return lax.fori_loop(1, picks[block], one_part, carry)

    lax.fori_loop(0, blocks, pick_block, 0)

    for expert in range(4):
        if expert < 2:
            fetch(expert + 2)
        for copy in weight_copies(expert):
            copy.wait()

        def one_tile(tile, carry, expert=expert):
            at = pl.ds(pl.multiple_of(tile * TILE, TILE), TILE)
            held = rows_ref[expert, at, :]
            turned = (((1,), (1,)), ((), ()))
            gated = lax.dot_general(held, gate_ref[expert], turned, preferred_element_type=F32)
            raised = lax.dot_general(held, up_ref[expert], turned, preferred_element_type=F32)
            hidden = (gated / (1.0 + jnp.exp(-gated)) * raised).astype(BF16)
            rows_ref[expert, at, :] = jnp.dot(
                hidden, down_ref[expert], preferred_element_type=F32
            ).astype(BF16)
            return carry

        lax.fori_loop(0, tiles[expert], one_tile, 0)

    def sum_block(block, carry):
        share = shares[block]

        def one_part(part):
            masks = mask_of(block, part)
            weight = jnp.concatenate([masks[e] * share[e : e + 1, :] for e in range(4)])
            high = weight.astype(BF16)
            low = (weight - high.astype(F32)).astype(BF16)
            made = jnp.concatenate([rows_ref[e, place(e, block, part), :] for e in range(4)])
            dims = (((0,), (0,)), ((), ()))
            return lax.dot_general(
                high, made, dims, preferred_element_type=F32
            ) + lax.dot_general(low, made, dims, preferred_element_type=F32)

        out_ref[block] = one_part(0).astype(BF16)

        @pl.when(picks[block] > 1)
        def _():
            sum_ref[...] = one_part(0)

            def add_part(part, carry):
                sum_ref[...] += one_part(part)
                return carry

            lax.fori_loop(1, picks[block], add_part, 0)
            out_ref[block] = sum_ref[...].astype(BF16)

        when_at(block, lambda each: save(each).start())
        return carry

    lax.fori_loop(0, blocks, sum_block, 0)
    for block in range(blocks):
        save(block).wait()


def run_experts(starts, picks, tiles, pieces, ranks, shares, own, other):
    features = pieces[0].shape[1]
    hidden = own[0].shape[1]
    blocks = ranks.shape[0]
    tokens = blocks * BLOCK
    anywhere = pl.BlockSpec(memory_space=pl.ANY)
    whole = pl.BlockSpec(ranks.shape, lambda *_: (0, 0, 0))
    return pl.pallas_call(
        expert_kernel,
        grid_spec=pltpu.PrefetchScalarGridSpec(
            num_scalar_prefetch=3,
            grid=(1,),
            in_specs=[anywhere] * 5 + [whole] * 2 + [anywhere] * 6,
            out_specs=[anywhere] * 5,
            scratch_shapes=[
                pltpu.VMEM((4, tokens + TILE, features), BF16),
                pltpu.VMEM((4, hidden, features), BF16),
                pltpu.VMEM((4, hidden, features), BF16),
                pltpu.VMEM((4, hidden, features), BF16),
                pltpu.VMEM((blocks, BLOCK, features), BF16),
                pltpu.VMEM((blocks, BLOCK, features), BF16),
                pltpu.VMEM((BLOCK, features), F32),
                pltpu.SemaphoreType.DMA((blocks,)),
                pltpu.SemaphoreType.DMA((blocks,)),
                pltpu.SemaphoreType.DMA((4, 3)),
            ],
        ),
        out_shape=[jax.ShapeDtypeStruct(piece.shape, BF16) for piece in pieces],
        compiler_params=pltpu.CompilerParams(vmem_limit_bytes=56 * 1024 * 1024),
        cost_estimate=pl.CostEstimate(
            flops=8 * tokens * features * hidden, bytes_accessed=26_000_000, transcendentals=0
        ),
    )(starts, picks, tiles, *pieces, ranks, shares, *own, *other)


def body(policy_states, row_lengths, send_order, expert_ids, gate_codes, w_gate, w_up, w_down):
    features = policy_states.shape[3]
    maxlen = policy_states.shape[2]
    top = expert_ids.shape[-1]
    x, y, core = (lax.axis_index(name) for name in PLANE)
    column = (x * 4 + y) * 2 + core
    device = lax.axis_index("dp") * 32 + column
    swap = [(0, 1), (1, 0)]
    own = [jnp.swapaxes(w_gate, 1, 2), jnp.swapaxes(w_up, 1, 2), w_down]
    other = [lax.ppermute(w, "core", swap) for w in own]

    packed = jnp.concatenate([row_lengths, send_order])
    spread = lax.all_to_all(
        jnp.broadcast_to(packed[None], (32, 16)), PLANE, 0, 0, tiled=True
    )
    lengths = spread[:, :8].T.reshape(256)
    held_by = (spread[:, 8:].T * 32 + jnp.arange(32, dtype=I32)[None, :]).reshape(256)
    every = jnp.arange(256, dtype=I32)
    offsets = jnp.sum(jnp.where(every[None, :] < every[:, None], lengths[None, :], 0), axis=1)
    is_holder = held_by[:, None] == every[None, :]
    judge_offsets = jnp.sum(jnp.where(is_holder, offsets[None, :], 0), axis=1)
    judge_lengths = jnp.sum(jnp.where(is_holder, lengths[None, :], 0), axis=1)
    at_me = every == device
    mine = jnp.sum(jnp.where(at_me, offsets, 0))
    judged_at = jnp.sum(jnp.where(at_me, judge_offsets, 0))
    judged_len = jnp.sum(jnp.where(at_me, judge_lengths, 0))

    pairs = jnp.arange(2 * 256, dtype=I32)
    peer, turn = pairs // 2, pairs % 2
    positions = jnp.arange(maxlen, dtype=I32)
    sent = lambda offset: (peer - offset) % 256 + 256 * turn
    rows = pick(one_hot(sent(mine), positions), policy_states.reshape(maxlen, features))
    names = jnp.concatenate(
        [
            expert_ids.reshape(maxlen, top).astype(BF16),
            gate_codes.reshape(maxlen, top).astype(BF16),
            jnp.zeros((maxlen, 128 - 2 * top), BF16),
        ],
        axis=1,
    )
    names = pick(one_hot(sent(judged_at), positions), names)
    outbound = jnp.concatenate([rows, names], axis=1).reshape(256, 2, features + 128)
    inbound = lax.all_to_all(outbound, ALL, 0, 0, tiled=True)
    inbound, *other = together([inbound, *other])
    inbound = inbound.reshape(512, features + 128)

    def slots_of(offset, length):
        offset, length = jnp.repeat(offset, 2), jnp.repeat(length, 2)
        position = (device - offset) % 256 + 256 * turn
        return jnp.where(position < length, (offset + position) // 256, -1)

    to_slot = one_hot(every, slots_of(offsets, lengths))
    judge_slot = one_hot(every, slots_of(judge_offsets, judge_lengths))
    states = pick(to_slot, inbound[:, :features])
    named = lax.dot_general(
        inbound[:, features : features + 16], judge_slot, (((0,), (1,)), ((), ())),
        preferred_element_type=F32,
    ).astype(BF16)

    experts = jnp.stack([2 * column, 2 * column + 1, 2 * (column ^ 1), 2 * (column ^ 1) + 1])
    below = (jnp.arange(BLOCK)[:, None] < jnp.arange(BLOCK)[None, :]).astype(BF16)
    size = 256 // CHUNKS
    blocks = 16 * size // BLOCK
    gathered, all_named = gather_plane(states[:size], states[size:], named)
    all_named = from_here(from_here(all_named, "x", 0), "y", 1)
    made, across = [], []
    for chunk in range(CHUNKS):
        named_here = all_named[..., chunk * size : (chunk + 1) * size]
        named_here = named_here.transpose(((2, 1, 0, 3), (2, 0, 1, 3))[chunk]).reshape(16, 16 * size)
        codes = named_here[top : 2 * top].astype(F32)
        share = codes / jnp.sum(codes, axis=0, keepdims=True)
        hit = named_here[None, :top].astype(I32) == experts[:, None, None]
        mask = jnp.any(hit, axis=1)
        shares = jnp.sum(jnp.where(hit, share[None], 0.0), axis=1)
        mask = mask.reshape(4, blocks, BLOCK)
        rank = jnp.dot(
            mask.reshape(4 * blocks, BLOCK).astype(BF16), below, preferred_element_type=F32
        ).reshape(4, blocks, BLOCK)
        ranks = jnp.where(mask, rank, -1.0).transpose(1, 0, 2)
        shares = shares.reshape(4, blocks, BLOCK).transpose(1, 0, 2)
        count = jnp.sum(mask.astype(I32), axis=2)
        taken = (count + 15) // 16 * 16
        earlier = jnp.arange(blocks)[None, :] < jnp.arange(blocks)[:, None]
        starts = jnp.sum(jnp.where(earlier[None], taken[:, None, :], 0), axis=2)
        tiles = (jnp.sum(taken, axis=1) + TILE - 1) // TILE
        picks = jnp.max((count + PICK - 1) // PICK, axis=0)
        made.append(
            run_experts(
                starts.reshape(-1), picks, tiles, gathered[chunk], ranks, shares, own, other
            )
        )
        across.append(send_across(made[chunk], "yx"[chunk]))
    held = together([*across[0], *made[1]])
    across[0], made[1] = held[:2], held[2:]
    finished = [
        sum_last(sum_line(made[0], across[0], "y"), "x"),
        sum_last(sum_line(made[1], across[1], "x"), "y"),
    ]

    made = jnp.concatenate(finished)
    back = lax.dot_general(
        judge_slot, made, (((0,), (0,)), ((), ())), preferred_element_type=F32
    ).astype(BF16)
    back = lax.all_to_all(back.reshape(256, 2, features), ALL, 0, 0, tiled=True)
    found = jnp.where(
        positions < judged_len, (positions + judged_at) % 256 * 2 + positions // 256, -1
    )
    result = pick(one_hot(found, pairs), back.reshape(512, features))
    return result.reshape(1, maxlen, features)


def solution(mesh):
    fine = Mesh(mesh.devices.reshape(8, 4, 4, 2), ALL)
    in_specs = (
        P(PLANE, "dp", None, None),
        P(PLANE),
        P(PLANE),
        P("dp", PLANE, None, None),
        P("dp", PLANE, None, None),
        P(PLANE, None, None),
        P(PLANE, None, None),
        P(PLANE, None, None),
    )
    return jax.shard_map(
        body, mesh=fine, in_specs=in_specs, out_specs=P(ALL, None, None), check_vma=False
    )
```

```python
import functools

import jax
import jax.numpy as jnp
from jax import lax
from jax.experimental import pallas as pl
from jax.experimental.pallas import tpu as pltpu
from jax.sharding import Mesh, PartitionSpec as P

F32 = jnp.float32
BF16 = jnp.bfloat16
I32 = jnp.int32
ALL = ("dp", "x", "y", "core")
PLANE = ("x", "y", "core")
BLOCK = 256
PICK = 64


def one_hot(rows, columns):
    return (rows[:, None] == columns[None, :]).astype(BF16)


def pick(matrix, values):
    return jnp.dot(matrix, values, preferred_element_type=F32).astype(BF16)


def shift(value, axis, by):
    size = lax.axis_size(axis)
    return lax.ppermute(value, axis, [(i, (i + by) % size) for i in range(size)])


def together(values):
    return list(lax.optimization_barrier(tuple(values)))


def add(*values):
    return sum(value.astype(F32) for value in values).astype(BF16)


def gather_near(one, two, named):
    steps = (-1, -2, 1)
    lines = [shift(one, "x", by) for by in steps] + [shift(two, "y", by) for by in steps]
    lines[0], named = together([lines[0], named])
    named = lax.all_to_all(
        jnp.broadcast_to(named[None], (16, *named.shape)), ("x", "y"), 0, 0, tiled=True
    ).reshape(4, 4, *named.shape)
    lines = together(lines)
    one, two = together([jnp.concatenate([one, *lines[:3]]), jnp.concatenate([two, *lines[3:]])])
    near = together([shift(v, axis, by) for v, axis in ((one, "y"), (two, "x")) for by in (-1, 1)])
    return (one, near[0], near[1]), (two, near[2], near[3]), named


def gather_far(one, two):
    half = one[0].shape[0] // 2
    return [
        shift(one[1][:half], "y", -1),
        shift(one[2][half:], "y", 1),
        shift(two[1][:half], "x", -1),
        shift(two[2][half:], "x", 1),
    ]


def sum_plane(one, two, across):
    half = one[0].shape[0] // 2
    sent = []
    for (_, after, before), low, high in ((one, *across[:2]), (two, *across[2:])):
        sent.append(add(before, jnp.pad(low, ((0, half), (0, 0)))))
        sent.append(add(after, jnp.pad(high, ((half, 0), (0, 0)))))
    found = together(
        [shift(sent[2 * i + j], axis, by) for i, axis in enumerate("yx") for j, by in ((0, -1), (1, 1))]
    )
    lines = [add(one[0], *found[:2]), add(two[0], *found[2:])]
    size = half // 2
    cut = together([line[i * size : (i + 1) * size] for line in lines for i in range(4)])
    found = together(
        [shift(cut[4 * j + i], axis, by) for j, axis in enumerate("xy") for i, by in ((1, 1), (2, 2), (3, -1))]
    )
    return [add(cut[0], *found[:3]), add(cut[4], *found[3:])]


def from_here(value, axis, dim):
    twice = jnp.concatenate([value, value], dim)
    return lax.dynamic_slice_in_dim(twice, lax.axis_index(axis), value.shape[dim], dim)


def tile_rows(blocks):
    return (blocks * 36 + 15) // 16 * 16


def expert_kernel(count, starts, picks, tiles, *refs):
    pieces, (ranks, shares), weights, outs, scratch = (
        refs[:count], refs[count : count + 2], refs[count + 2 : count + 8],
        refs[count + 8 : 2 * count + 8], refs[2 * count + 8 :],
    )
    gate0, up0, down0, gate1, up1, down1 = weights
    rows_ref, gate_ref, up_ref, down_ref, in_ref, out_ref, sum_ref = scratch[:7]
    in_sems, out_sems, w_sems = scratch[7:]
    blocks = ranks.shape[0]

    tile = tile_rows(blocks)
    spots = [(i, at) for i in range(count) for at in range(pieces[i].shape[0] // BLOCK)]

    def part_of(refs, block):
        piece, at = spots[block]
        return refs[piece].at[pl.ds(at * BLOCK, BLOCK)]

    def load(block):
        return pltpu.make_async_copy(part_of(pieces, block), in_ref.at[block], in_sems.at[block])

    def save(block):
        return pltpu.make_async_copy(out_ref.at[block], part_of(outs, block), out_sems.at[block])

    def when_at(block, action):
        for each in range(blocks):
            pl.when(block == each)(functools.partial(action, each))

    def weight_copies(expert):
        gate, up, down = ((gate0, up0, down0), (gate1, up1, down1))[expert // 2]
        return [
            pltpu.make_async_copy(w.at[expert % 2], ref.at[expert], w_sems.at[expert, i])
            for i, (w, ref) in enumerate(((gate, gate_ref), (up, up_ref), (down, down_ref)))
        ]

    def mask_of(block, part):
        lane_rank = ranks[block]
        wanted = (lax.broadcasted_iota(I32, (PICK, BLOCK), 0) + part * PICK).astype(F32)
        return [jnp.where(lane_rank[e : e + 1, :] == wanted, 1.0, 0.0) for e in range(4)]

    def place(expert, block, part):
        return pl.ds(pl.multiple_of(starts[expert * blocks + block] + part * PICK, 16), PICK)

    for block in range(blocks):
        load(block).start()

    def fetch(expert):
        for copy in weight_copies(expert):
            copy.start()

    def pick_block(block, carry):
        when_at(block, lambda each: load(each).wait())
        pl.when(block == 0)(functools.partial(fetch, 0))
        pl.when(block == blocks // 2)(functools.partial(fetch, 1))

        def one_part(part, carry):
            mask = jnp.concatenate(mask_of(block, part)).astype(BF16)
            got = jnp.dot(mask, in_ref[block], preferred_element_type=F32).astype(BF16)
            for e in range(4):
                rows_ref[e, place(e, block, part), :] = got[e * PICK : (e + 1) * PICK]
            return carry

        one_part(0, 0)
        return lax.fori_loop(1, picks[block], one_part, carry)

    lax.fori_loop(0, blocks, pick_block, 0)

    for expert in range(4):
        if expert < 2:
            fetch(expert + 2)
        for copy in weight_copies(expert):
            copy.wait()

        def one_tile(i, carry, expert=expert):
            at = pl.ds(pl.multiple_of(i * tile, 16), tile)
            held = rows_ref[expert, at, :]
            turned = (((1,), (1,)), ((), ()))
            gated = lax.dot_general(held, gate_ref[expert], turned, preferred_element_type=F32)
            raised = lax.dot_general(held, up_ref[expert], turned, preferred_element_type=F32)
            hidden = (gated / (1.0 + jnp.exp(-gated)) * raised).astype(BF16)
            rows_ref[expert, at, :] = jnp.dot(
                hidden, down_ref[expert], preferred_element_type=F32
            ).astype(BF16)
            return carry

        lax.fori_loop(0, tiles[expert], one_tile, 0)

    def sum_block(block, carry):
        share = shares[block]

        def one_part(part):
            masks = mask_of(block, part)
            weight = jnp.concatenate([masks[e] * share[e : e + 1, :] for e in range(4)])
            high = weight.astype(BF16)
            low = (weight - high.astype(F32)).astype(BF16)
            made = jnp.concatenate([rows_ref[e, place(e, block, part), :] for e in range(4)])
            dims = (((0,), (0,)), ((), ()))
            return lax.dot_general(
                high, made, dims, preferred_element_type=F32
            ) + lax.dot_general(low, made, dims, preferred_element_type=F32)

        out_ref[block] = one_part(0).astype(BF16)

        @pl.when(picks[block] > 1)
        def _():
            sum_ref[...] = one_part(0)

            def add_part(part, carry):
                sum_ref[...] += one_part(part)
                return carry

            lax.fori_loop(1, picks[block], add_part, 0)
            out_ref[block] = sum_ref[...].astype(BF16)

        when_at(block, lambda each: save(each).start())
        return carry

    lax.fori_loop(0, blocks, sum_block, 0)
    for block in range(blocks):
        save(block).wait()


def run_experts(starts, picks, tiles, pieces, ranks, shares, own, other):
    features = pieces[0].shape[1]
    hidden = own[0].shape[1]
    blocks = ranks.shape[0]
    count = len(pieces)
    tokens = blocks * BLOCK
    capacity = tokens + max(BLOCK, tile_rows(blocks))
    anywhere = pl.BlockSpec(memory_space=pl.ANY)
    whole = pl.BlockSpec(ranks.shape, lambda *_: (0, 0, 0))
    return pl.pallas_call(
        functools.partial(expert_kernel, count),
        grid_spec=pltpu.PrefetchScalarGridSpec(
            num_scalar_prefetch=3,
            grid=(1,),
            in_specs=[anywhere] * count + [whole] * 2 + [anywhere] * 6,
            out_specs=[anywhere] * count,
            scratch_shapes=[
                pltpu.VMEM((4, capacity, features), BF16),
                pltpu.VMEM((4, hidden, features), BF16),
                pltpu.VMEM((4, hidden, features), BF16),
                pltpu.VMEM((4, hidden, features), BF16),
                pltpu.VMEM((blocks, BLOCK, features), BF16),
                pltpu.VMEM((blocks, BLOCK, features), BF16),
                pltpu.VMEM((BLOCK, features), F32),
                pltpu.SemaphoreType.DMA((blocks,)),
                pltpu.SemaphoreType.DMA((blocks,)),
                pltpu.SemaphoreType.DMA((4, 3)),
            ],
        ),
        out_shape=[jax.ShapeDtypeStruct(piece.shape, BF16) for piece in pieces],
        compiler_params=pltpu.CompilerParams(vmem_limit_bytes=56 * 1024 * 1024),
        cost_estimate=pl.CostEstimate(
            flops=8 * tokens * features * hidden, bytes_accessed=26_000_000, transcendentals=0
        ),
    )(starts, picks, tiles, *pieces, ranks, shares, *own, *other)


def body(policy_states, row_lengths, send_order, expert_ids, gate_codes, w_gate, w_up, w_down):
    features = policy_states.shape[3]
    maxlen = policy_states.shape[2]
    top = expert_ids.shape[-1]
    x, y, core = (lax.axis_index(name) for name in PLANE)
    column = (x * 4 + y) * 2 + core
    device = lax.axis_index("dp") * 32 + column
    swap = [(0, 1), (1, 0)]
    own = [jnp.swapaxes(w_gate, 1, 2), jnp.swapaxes(w_up, 1, 2), w_down]
    other = [lax.ppermute(w, "core", swap) for w in own]

    packed = jnp.concatenate([row_lengths, send_order])
    spread = lax.all_to_all(
        jnp.broadcast_to(packed[None], (32, 16)), PLANE, 0, 0, tiled=True
    )
    lengths = spread[:, :8].T.reshape(256)
    held_by = (spread[:, 8:].T * 32 + jnp.arange(32, dtype=I32)[None, :]).reshape(256)
    every = jnp.arange(256, dtype=I32)
    offsets = jnp.sum(jnp.where(every[None, :] < every[:, None], lengths[None, :], 0), axis=1)
    is_holder = held_by[:, None] == every[None, :]
    judge_offsets = jnp.sum(jnp.where(is_holder, offsets[None, :], 0), axis=1)
    judge_lengths = jnp.sum(jnp.where(is_holder, lengths[None, :], 0), axis=1)
    at_me = every == device
    mine = jnp.sum(jnp.where(at_me, offsets, 0))
    judged_at = jnp.sum(jnp.where(at_me, judge_offsets, 0))
    judged_len = jnp.sum(jnp.where(at_me, judge_lengths, 0))

    pairs = jnp.arange(2 * 256, dtype=I32)
    peer, turn = pairs // 2, pairs % 2
    positions = jnp.arange(maxlen, dtype=I32)
    sent = lambda offset: (peer - offset) % 256 + 256 * turn
    rows = pick(one_hot(sent(mine), positions), policy_states.reshape(maxlen, features))
    names = jnp.concatenate(
        [
            expert_ids.reshape(maxlen, top).astype(BF16),
            gate_codes.reshape(maxlen, top).astype(BF16),
            jnp.zeros((maxlen, 128 - 2 * top), BF16),
        ],
        axis=1,
    )
    names = pick(one_hot(sent(judged_at), positions), names)
    outbound = jnp.concatenate([rows, names], axis=1).reshape(256, 2, features + 128)
    inbound = lax.all_to_all(outbound, ALL, 0, 0, tiled=True)
    inbound, *other = together([inbound, *other])
    inbound = inbound.reshape(512, features + 128)

    def slots_of(offset, length):
        offset, length = jnp.repeat(offset, 2), jnp.repeat(length, 2)
        position = (device - offset) % 256 + 256 * turn
        return jnp.where(position < length, (offset + position) // 256, -1)

    to_slot = one_hot(every, slots_of(offsets, lengths))
    judge_slot = one_hot(every, slots_of(judge_offsets, judge_lengths))
    states = pick(to_slot, inbound[:, :features])
    named = lax.dot_general(
        inbound[:, features : features + 16], judge_slot, (((0,), (1,)), ((), ())),
        preferred_element_type=F32,
    ).astype(BF16)

    experts = jnp.stack([2 * column, 2 * column + 1, 2 * (column ^ 1), 2 * (column ^ 1) + 1])
    below = (jnp.arange(BLOCK)[:, None] < jnp.arange(BLOCK)[None, :]).astype(BF16)

    def judge(pieces, named_here):
        blocks = named_here.shape[1] // BLOCK
        codes = named_here[top : 2 * top].astype(F32)
        share = codes / jnp.sum(codes, axis=0, keepdims=True)
        hit = named_here[None, :top].astype(I32) == experts[:, None, None]
        mask = jnp.any(hit, axis=1)
        shares = jnp.sum(jnp.where(hit, share[None], 0.0), axis=1)
        mask = mask.reshape(4, blocks, BLOCK)
        rank = jnp.dot(
            mask.reshape(4 * blocks, BLOCK).astype(BF16), below, preferred_element_type=F32
        ).reshape(4, blocks, BLOCK)
        ranks = jnp.where(mask, rank, -1.0).transpose(1, 0, 2)
        shares = shares.reshape(4, blocks, BLOCK).transpose(1, 0, 2)
        count = jnp.sum(mask.astype(I32), axis=2)
        taken = (count + 15) // 16 * 16
        earlier = jnp.arange(blocks)[None, :] < jnp.arange(blocks)[:, None]
        starts = jnp.sum(jnp.where(earlier[None], taken[:, None, :], 0), axis=2)
        tile = tile_rows(blocks)
        tiles = (jnp.sum(taken, axis=1) + tile - 1) // tile
        picks = jnp.max((count + PICK - 1) // PICK, axis=0)
        return run_experts(starts.reshape(-1), picks, tiles, pieces, ranks, shares, own, other)

    one, two, all_named = gather_near(states[:128], states[128:], named)
    all_named = from_here(from_here(all_named, "x", 0), "y", 1)
    named_one = all_named[..., :128].transpose(2, 1, 0, 3).reshape(16, 4, 512)
    named_two = all_named[..., 128:].transpose(2, 0, 1, 3).reshape(16, 4, 512)
    near_of = lambda value: jnp.concatenate([value[:, 0], value[:, 1], value[:, 3]], axis=1)
    far = gather_far(one, two)
    one_made = judge(one, near_of(named_one))
    held = together([*far, *one_made])
    far, one_made = held[:4], held[4:]
    far_made = judge(far, jnp.concatenate([named_one[:, 2], named_two[:, 2]], axis=1))
    held = together([*far_made, *two])
    far_made, two = held[:4], held[4:]
    across = [
        shift(far_made[0], "y", -1),
        shift(far_made[1], "y", 1),
        shift(far_made[2], "x", -1),
        shift(far_made[3], "x", 1),
    ]
    two_made = judge(two, near_of(named_two))
    held = together([*across, *two_made])
    finished = sum_plane(one_made, held[4:], held[:4])

    made = jnp.concatenate(finished)
    back = lax.dot_general(
        judge_slot, made, (((0,), (0,)), ((), ())), preferred_element_type=F32
    ).astype(BF16)
    back = lax.all_to_all(back.reshape(256, 2, features), ALL, 0, 0, tiled=True)
    found = jnp.where(
        positions < judged_len, (positions + judged_at) % 256 * 2 + positions // 256, -1
    )
    result = pick(one_hot(found, pairs), back.reshape(512, features))
    return result.reshape(1, maxlen, features)


def solution(mesh):
    fine = Mesh(mesh.devices.reshape(8, 4, 4, 2), ALL)
    in_specs = (
        P(PLANE, "dp", None, None),
        P(PLANE),
        P(PLANE),
        P("dp", PLANE, None, None),
        P("dp", PLANE, None, None),
        P(PLANE, None, None),
        P(PLANE, None, None),
        P(PLANE, None, None),
    )
    return jax.shard_map(
        body, mesh=fine, in_specs=in_specs, out_specs=P(ALL, None, None), check_vma=False
    )
```

```python
import functools

import jax
import jax.numpy as jnp
from jax import lax
from jax.experimental import pallas as pl
from jax.experimental.pallas import tpu as pltpu
from jax.sharding import Mesh, PartitionSpec as P

F32 = jnp.float32
BF16 = jnp.bfloat16
I32 = jnp.int32
ALL = ("dp", "x", "y", "core")
PLANE = ("x", "y", "core")
BLOCK = 256
PICK = 64


def one_hot(rows, columns):
    return (rows[:, None] == columns[None, :]).astype(BF16)


def pick(matrix, values):
    return jnp.dot(matrix, values, preferred_element_type=F32).astype(BF16)


def shift(value, axis, by):
    size = lax.axis_size(axis)
    return lax.ppermute(value, axis, [(i, (i + by) % size) for i in range(size)])


def together(values):
    return list(lax.optimization_barrier(tuple(values)))


def add(*values):
    return sum(value.astype(F32) for value in values).astype(BF16)


def gather_near(one, two, named):
    steps = (-1, -2, 1)
    lines = [shift(one, "x", by) for by in steps] + [shift(two, "y", by) for by in steps]
    lines[0], named = together([lines[0], named])
    named = lax.all_to_all(
        jnp.broadcast_to(named[None], (16, *named.shape)), ("x", "y"), 0, 0, tiled=True
    ).reshape(4, 4, *named.shape)
    *lines, named = together([*lines, named])
    one, two = together([jnp.concatenate([one, *lines[:3]]), jnp.concatenate([two, *lines[3:]])])
    near = together([shift(v, axis, by) for v, axis in ((one, "y"), (two, "x")) for by in (-1, 1)])
    return (one, near[0], near[1]), (two, near[2], near[3]), named


def gather_far(one, two):
    half = one[0].shape[0] // 2
    return [
        shift(one[1][:half], "y", -1),
        shift(one[2][half:], "y", 1),
        shift(two[1][:half], "x", -1),
        shift(two[2][half:], "x", 1),
    ]


def sum_plane(one, two, across):
    half = one[0].shape[0] // 2
    sent = []
    for (_, after, before), low, high in ((one, *across[:2]), (two, *across[2:])):
        sent.append(add(before, jnp.pad(low, ((0, half), (0, 0)))))
        sent.append(add(after, jnp.pad(high, ((half, 0), (0, 0)))))
    found = together(
        [shift(sent[2 * i + j], axis, by) for i, axis in enumerate("yx") for j, by in ((0, -1), (1, 1))]
    )
    lines = [add(one[0], *found[:2]), add(two[0], *found[2:])]
    size = half // 2
    cut = together([line[i * size : (i + 1) * size] for line in lines for i in range(4)])
    found = together(
        [shift(cut[4 * j + i], axis, by) for j, axis in enumerate("xy") for i, by in ((1, 1), (2, 2), (3, -1))]
    )
    return [add(cut[0], *found[:3]), add(cut[4], *found[3:])]


def from_here(value, axis, dim):
    twice = jnp.concatenate([value, value], dim)
    return lax.dynamic_slice_in_dim(twice, lax.axis_index(axis), value.shape[dim], dim)


def tile_rows(blocks):
    return (blocks * 36 + 15) // 16 * 16


def expert_kernel(count, starts, picks, tiles, *refs):
    pieces, (ranks, shares), weights, outs, scratch = (
        refs[:count], refs[count : count + 2], refs[count + 2 : count + 8],
        refs[count + 8 : 2 * count + 8], refs[2 * count + 8 :],
    )
    gate0, up0, down0, gate1, up1, down1 = weights
    rows_ref, held_ref, sum_ref, in_sems, out_sems = scratch
    blocks = ranks.shape[0]

    tile = tile_rows(blocks)
    spots = [(i, at) for i in range(count) for at in range(pieces[i].shape[0] // BLOCK)]

    def part_of(refs, block):
        piece, at = spots[block]
        return refs[piece].at[pl.ds(at * BLOCK, BLOCK)]

    def load(block):
        return pltpu.make_async_copy(part_of(pieces, block), held_ref.at[block], in_sems.at[block])

    def save(block):
        return pltpu.make_async_copy(held_ref.at[block], part_of(outs, block), out_sems.at[block])

    def when_at(block, action):
        for each in range(blocks):
            pl.when(block == each)(functools.partial(action, each))

    def weights_of(expert):
        gate, up, down = ((gate0, up0, down0), (gate1, up1, down1))[expert // 2]
        return gate.at[expert % 2], up.at[expert % 2], down.at[expert % 2]

    def mask_of(block, part):
        lane_rank = ranks[block]
        wanted = (lax.broadcasted_iota(I32, (PICK, BLOCK), 0) + part * PICK).astype(F32)
        return [jnp.where(lane_rank[e : e + 1, :] == wanted, 1.0, 0.0) for e in range(4)]

    def place(expert, block, part):
        return pl.ds(pl.multiple_of(starts[expert * blocks + block] + part * PICK, 16), PICK)

    for block in range(blocks):
        load(block).start()

    def pick_block(block, carry):
        when_at(block, lambda each: load(each).wait())
        def one_part(part, carry):
            mask = jnp.concatenate(mask_of(block, part)).astype(BF16)
            got = jnp.dot(mask, held_ref[block], preferred_element_type=F32).astype(BF16)
            for e in range(4):
                rows_ref[e, place(e, block, part), :] = got[e * PICK : (e + 1) * PICK]
            return carry

        one_part(0, 0)
        return lax.fori_loop(1, picks[block], one_part, carry)

    lax.fori_loop(0, blocks, pick_block, 0)

    for expert in range(4):
        gate, up, down = weights_of(expert)

        def one_tile(i, carry, expert=expert, gate=gate, up=up, down=down):
            at = pl.ds(pl.multiple_of(i * tile, 16), tile)
            held = rows_ref[expert, at, :]
            turned = (((1,), (1,)), ((), ()))
            gated = lax.dot_general(held, gate[...], turned, preferred_element_type=F32)
            raised = lax.dot_general(held, up[...], turned, preferred_element_type=F32)
            hidden = (gated / (1.0 + jnp.exp(-gated)) * raised).astype(BF16)
            rows_ref[expert, at, :] = jnp.dot(
                hidden, down[...], preferred_element_type=F32
            ).astype(BF16)
            return carry

        lax.fori_loop(0, tiles[expert], one_tile, 0)

    def sum_block(block, carry):
        share = shares[block]

        def one_part(part):
            masks = mask_of(block, part)
            weight = jnp.concatenate([masks[e] * share[e : e + 1, :] for e in range(4)])
            high = weight.astype(BF16)
            low = (weight - high.astype(F32)).astype(BF16)
            made = jnp.concatenate([rows_ref[e, place(e, block, part), :] for e in range(4)])
            dims = (((0,), (0,)), ((), ()))
            return lax.dot_general(
                high, made, dims, preferred_element_type=F32
            ) + lax.dot_general(low, made, dims, preferred_element_type=F32)

        held_ref[block] = one_part(0).astype(BF16)

        @pl.when(picks[block] > 1)
        def _():
            sum_ref[...] = one_part(0)

            def add_part(part, carry):
                sum_ref[...] += one_part(part)
                return carry

            lax.fori_loop(1, picks[block], add_part, 0)
            held_ref[block] = sum_ref[...].astype(BF16)

        when_at(block, lambda each: save(each).start())
        return carry

    lax.fori_loop(0, blocks, sum_block, 0)
    for block in range(blocks):
        save(block).wait()


def run_experts(starts, picks, tiles, pieces, ranks, shares, own, other):
    features = pieces[0].shape[1]
    hidden = own[0].shape[1]
    blocks = ranks.shape[0]
    count = len(pieces)
    tokens = blocks * BLOCK
    capacity = tokens + max(BLOCK, tile_rows(blocks))
    anywhere = pl.BlockSpec(memory_space=pl.ANY)
    whole = pl.BlockSpec(ranks.shape, lambda *_: (0, 0, 0))
    return pl.pallas_call(
        functools.partial(expert_kernel, count),
        grid_spec=pltpu.PrefetchScalarGridSpec(
            num_scalar_prefetch=3,
            grid=(1,),
            in_specs=[anywhere] * count + [whole] * 2 + [pl.BlockSpec(memory_space=pltpu.VMEM)] * 6,
            out_specs=[anywhere] * count,
            scratch_shapes=[
                pltpu.VMEM((4, capacity, features), BF16),
                pltpu.VMEM((blocks, BLOCK, features), BF16),
                pltpu.VMEM((BLOCK, features), F32),
                pltpu.SemaphoreType.DMA((blocks,)),
                pltpu.SemaphoreType.DMA((blocks,)),
            ],
        ),
        out_shape=[jax.ShapeDtypeStruct(piece.shape, BF16) for piece in pieces],
        compiler_params=pltpu.CompilerParams(vmem_limit_bytes=30 * 1024 * 1024),
        cost_estimate=pl.CostEstimate(
            flops=8 * tokens * features * hidden, bytes_accessed=26_000_000, transcendentals=0
        ),
    )(starts, picks, tiles, *pieces, ranks, shares, *own, *other)


def body(policy_states, row_lengths, send_order, expert_ids, gate_codes, w_gate, w_up, w_down):
    features = policy_states.shape[3]
    maxlen = policy_states.shape[2]
    top = expert_ids.shape[-1]
    x, y, core = (lax.axis_index(name) for name in PLANE)
    column = (x * 4 + y) * 2 + core
    device = lax.axis_index("dp") * 32 + column
    swap = [(0, 1), (1, 0)]
    own = [jnp.swapaxes(w_gate, 1, 2), jnp.swapaxes(w_up, 1, 2), w_down]
    other = [lax.ppermute(w, "core", swap) for w in own]

    packed = jnp.concatenate([row_lengths, send_order])
    spread = lax.all_to_all(
        jnp.broadcast_to(packed[None], (32, 16)), PLANE, 0, 0, tiled=True
    )
    lengths = spread[:, :8].T.reshape(256)
    held_by = (spread[:, 8:].T * 32 + jnp.arange(32, dtype=I32)[None, :]).reshape(256)
    every = jnp.arange(256, dtype=I32)
    offsets = jnp.sum(jnp.where(every[None, :] < every[:, None], lengths[None, :], 0), axis=1)
    is_holder = held_by[:, None] == every[None, :]
    judge_offsets = jnp.sum(jnp.where(is_holder, offsets[None, :], 0), axis=1)
    judge_lengths = jnp.sum(jnp.where(is_holder, lengths[None, :], 0), axis=1)
    my_holder = jnp.sum(jnp.where(every == device, held_by, 0))
    mine = jnp.sum(jnp.where(every < device, lengths, 0))
    judged_at = jnp.sum(jnp.where(every < my_holder, lengths, 0))
    judged_len = jnp.sum(jnp.where(every == my_holder, lengths, 0))

    pairs = jnp.arange(2 * 256, dtype=I32)
    peer, turn = pairs // 2, pairs % 2
    positions = jnp.arange(maxlen, dtype=I32)
    sent = lambda offset: (peer - offset) % 256 + 256 * turn
    rows = pick(one_hot(sent(mine), positions), policy_states.reshape(maxlen, features))
    names = jnp.concatenate(
        [
            expert_ids.reshape(maxlen, top).astype(BF16),
            gate_codes.reshape(maxlen, top).astype(BF16),
            jnp.zeros((maxlen, 128 - 2 * top), BF16),
        ],
        axis=1,
    )
    names = pick(one_hot(sent(judged_at), positions), names)
    outbound = jnp.concatenate([rows, names], axis=1).reshape(256, 2, features + 128)
    inbound = lax.all_to_all(outbound, ALL, 0, 0, tiled=True)
    inbound, *other = together([inbound, *other])
    own, other = (
        [pltpu.with_memory_space_constraint(w, pltpu.VMEM) for w in ws] for ws in (own, other)
    )
    inbound = inbound.reshape(512, features + 128)

    def slots_of(offset, length):
        offset, length = jnp.repeat(offset, 2), jnp.repeat(length, 2)
        position = (device - offset) % 256 + 256 * turn
        return jnp.where(position < length, (offset + position) // 256, -1)

    to_slot = one_hot(every, slots_of(offsets, lengths))
    judge_slot = one_hot(every, slots_of(judge_offsets, judge_lengths))
    states = pick(to_slot, inbound[:, :features])
    named = lax.dot_general(
        inbound[:, features : features + 16], judge_slot, (((0,), (1,)), ((), ())),
        preferred_element_type=F32,
    ).astype(BF16)

    experts = jnp.stack([2 * column, 2 * column + 1, 2 * (column ^ 1), 2 * (column ^ 1) + 1])
    below = (jnp.arange(BLOCK)[:, None] < jnp.arange(BLOCK)[None, :]).astype(BF16)

    def judge(pieces, named_here):
        blocks = named_here.shape[1] // BLOCK
        codes = named_here[top : 2 * top].astype(F32)
        share = codes / jnp.sum(codes, axis=0, keepdims=True)
        hit = named_here[None, :top].astype(I32) == experts[:, None, None]
        mask = jnp.any(hit, axis=1)
        shares = jnp.sum(jnp.where(hit, share[None], 0.0), axis=1)
        mask = mask.reshape(4, blocks, BLOCK)
        rank = jnp.dot(
            mask.reshape(4 * blocks, BLOCK).astype(BF16), below, preferred_element_type=F32
        ).reshape(4, blocks, BLOCK)
        ranks = jnp.where(mask, rank, -1.0).transpose(1, 0, 2)
        shares = shares.reshape(4, blocks, BLOCK).transpose(1, 0, 2)
        count = jnp.sum(mask.astype(I32), axis=2)
        taken = (count + 15) // 16 * 16
        earlier = jnp.arange(blocks)[None, :] < jnp.arange(blocks)[:, None]
        starts = jnp.sum(jnp.where(earlier[None], taken[:, None, :], 0), axis=2)
        tile = tile_rows(blocks)
        tiles = (jnp.sum(taken, axis=1) + tile - 1) // tile
        picks = jnp.max((count + PICK - 1) // PICK, axis=0)
        return run_experts(starts.reshape(-1), picks, tiles, pieces, ranks, shares, own, other)

    one, two, all_named = gather_near(states[:128], states[128:], named)
    all_named = from_here(from_here(all_named, "x", 0), "y", 1)
    named_one = all_named[..., :128].transpose(2, 1, 0, 3).reshape(16, 4, 512)
    named_two = all_named[..., 128:].transpose(2, 0, 1, 3).reshape(16, 4, 512)
    near_of = lambda value: jnp.concatenate([value[:, 0], value[:, 1], value[:, 3]], axis=1)
    far = gather_far(one, two)
    one_made = judge(one, near_of(named_one))
    held = together([*far, *one_made])
    far, one_made = held[:4], held[4:]
    far_made = judge(far, jnp.concatenate([named_one[:, 2], named_two[:, 2]], axis=1))
    held = together([*far_made, *two])
    far_made, two = held[:4], held[4:]
    across = [
        shift(far_made[0], "y", -1),
        shift(far_made[1], "y", 1),
        shift(far_made[2], "x", -1),
        shift(far_made[3], "x", 1),
    ]
    two_made = judge(two, near_of(named_two))
    held = together([*across, *two_made])
    finished = sum_plane(one_made, held[4:], held[:4])

    made = jnp.concatenate(finished)
    back = lax.dot_general(
        judge_slot, made, (((0,), (0,)), ((), ())), preferred_element_type=F32
    ).astype(BF16)
    back = lax.all_to_all(back.reshape(256, 2, features), ALL, 0, 0, tiled=True)
    found = jnp.where(
        positions < judged_len, (positions + judged_at) % 256 * 2 + positions // 256, -1
    )
    result = pick(one_hot(found, pairs), back.reshape(512, features))
    return result.reshape(1, maxlen, features)


def solution(mesh):
    fine = Mesh(mesh.devices.reshape(8, 4, 4, 2), ALL)
    in_specs = (
        P(PLANE, "dp", None, None),
        P(PLANE),
        P(PLANE),
        P("dp", PLANE, None, None),
        P("dp", PLANE, None, None),
        P(PLANE, None, None),
        P(PLANE, None, None),
        P(PLANE, None, None),
    )
    return jax.shard_map(
        body, mesh=fine, in_specs=in_specs, out_specs=P(ALL, None, None), check_vma=False
    )
```

```python
import functools

import jax
import jax.numpy as jnp
from jax import lax
from jax.experimental import pallas as pl
from jax.experimental.pallas import tpu as pltpu
from jax.sharding import Mesh, PartitionSpec as P

F32 = jnp.float32
BF16 = jnp.bfloat16
I32 = jnp.int32
ALL = ("dp", "x", "y", "core")
PLANE = ("x", "y", "core")
BLOCK = 256
PICK = 64


def one_hot(rows, columns):
    return (rows[:, None] == columns[None, :]).astype(BF16)


def pick(matrix, values):
    return jnp.dot(matrix, values, preferred_element_type=F32).astype(BF16)


def shift(value, axis, by):
    size = lax.axis_size(axis)
    return lax.ppermute(value, axis, [(i, (i + by) % size) for i in range(size)])


def together(values):
    return list(lax.optimization_barrier(tuple(values)))


def add(*values):
    return sum(value.astype(F32) for value in values).astype(BF16)


def gather_lines(one, two, named):
    steps = (-1, -2, 1)
    lines = [shift(one, "x", by) for by in steps] + [shift(two, "y", by) for by in steps]
    lines[0], named = together([lines[0], named])
    named = lax.all_to_all(
        jnp.broadcast_to(named[None], (16, *named.shape)), ("x", "y"), 0, 0, tiled=True
    ).reshape(4, 4, *named.shape)
    lines = together(lines)
    halves = together(
        [
            jnp.concatenate(pair)
            for pair in ((one, lines[0]), lines[1:3], (two, lines[3]), lines[4:6])
        ]
    )
    return halves, named


def last_sums(lines):
    size = lines[0].shape[0] // 2
    cut = together([line[i * size : (i + 1) * size] for line in lines for i in range(2)])
    found = together(
        [
            shift(cut[4 * j + i], axis, by)
            for j, axis in enumerate("xy")
            for i, by in ((1, 1), (2, 2), (3, -1))
        ]
    )
    return [add(cut[0], *found[:3]), add(cut[4], *found[3:])]


def from_here(value, axis, dim):
    twice = jnp.concatenate([value, value], dim)
    return lax.dynamic_slice_in_dim(twice, lax.axis_index(axis), value.shape[dim], dim)


def tile_rows(blocks):
    return (blocks * 36 + 15) // 16 * 16


def expert_kernel(count, starts, picks, tiles, *refs):
    pieces, (ranks, shares), weights, outs, scratch = (
        refs[:count], refs[count : count + 2], refs[count + 2 : count + 8],
        refs[count + 8 : 2 * count + 8], refs[2 * count + 8 :],
    )
    gate0, up0, down0, gate1, up1, down1 = weights
    rows_ref, gate_ref, up_ref, down_ref, in_ref, out_ref, sum_ref = scratch[:7]
    in_sems, out_sems, w_sems = scratch[7:]
    blocks = ranks.shape[0]

    tile = tile_rows(blocks)
    spots = [(i, at) for i in range(count) for at in range(pieces[i].shape[0] // BLOCK)]

    def part_of(refs, block):
        piece, at = spots[block]
        return refs[piece].at[pl.ds(at * BLOCK, BLOCK)]

    def load(block):
        return pltpu.make_async_copy(part_of(pieces, block), in_ref.at[block], in_sems.at[block])

    def save(block):
        return pltpu.make_async_copy(out_ref.at[block], part_of(outs, block), out_sems.at[block])

    def when_at(block, action):
        for each in range(blocks):
            pl.when(block == each)(functools.partial(action, each))

    def weight_copies(expert):
        gate, up, down = ((gate0, up0, down0), (gate1, up1, down1))[expert // 2]
        return [
            pltpu.make_async_copy(w.at[expert % 2], ref.at[expert], w_sems.at[expert, i])
            for i, (w, ref) in enumerate(((gate, gate_ref), (up, up_ref), (down, down_ref)))
        ]

    def mask_of(block, part):
        lane_rank = ranks[block]
        wanted = (lax.broadcasted_iota(I32, (PICK, BLOCK), 0) + part * PICK).astype(F32)
        return [jnp.where(lane_rank[e : e + 1, :] == wanted, 1.0, 0.0) for e in range(4)]

    def place(expert, block, part):
        return pl.ds(pl.multiple_of(starts[expert * blocks + block] + part * PICK, 16), PICK)

    for block in range(blocks):
        load(block).start()

    def fetch(expert):
        for copy in weight_copies(expert):
            copy.start()

    def pick_block(block, carry):
        when_at(block, lambda each: load(each).wait())
        pl.when(block == 0)(functools.partial(fetch, 0))
        pl.when(block == blocks // 2)(functools.partial(fetch, 1))

        def one_part(part, carry):
            mask = jnp.concatenate(mask_of(block, part)).astype(BF16)
            got = jnp.dot(mask, in_ref[block], preferred_element_type=F32).astype(BF16)
            for e in range(4):
                rows_ref[e, place(e, block, part), :] = got[e * PICK : (e + 1) * PICK]
            return carry

        one_part(0, 0)
        return lax.fori_loop(1, picks[block], one_part, carry)

    lax.fori_loop(0, blocks, pick_block, 0)

    for expert in range(4):
        if expert < 2:
            fetch(expert + 2)
        for copy in weight_copies(expert):
            copy.wait()

        def one_tile(i, carry, expert=expert):
            at = pl.ds(pl.multiple_of(i * tile, 16), tile)
            held = rows_ref[expert, at, :]
            turned = (((1,), (1,)), ((), ()))
            gated = lax.dot_general(held, gate_ref[expert], turned, preferred_element_type=F32)
            raised = lax.dot_general(held, up_ref[expert], turned, preferred_element_type=F32)
            hidden = (gated / (1.0 + jnp.exp(-gated)) * raised).astype(BF16)
            rows_ref[expert, at, :] = jnp.dot(
                hidden, down_ref[expert], preferred_element_type=F32
            ).astype(BF16)
            return carry

        lax.fori_loop(0, tiles[expert], one_tile, 0)

    def sum_block(block, carry):
        share = shares[block]

        def one_part(part):
            masks = mask_of(block, part)
            weight = jnp.concatenate([masks[e] * share[e : e + 1, :] for e in range(4)])
            high = weight.astype(BF16)
            low = (weight - high.astype(F32)).astype(BF16)
            made = jnp.concatenate([rows_ref[e, place(e, block, part), :] for e in range(4)])
            dims = (((0,), (0,)), ((), ()))
            return lax.dot_general(
                high, made, dims, preferred_element_type=F32
            ) + lax.dot_general(low, made, dims, preferred_element_type=F32)

        out_ref[block] = one_part(0).astype(BF16)

        @pl.when(picks[block] > 1)
        def _():
            sum_ref[...] = one_part(0)

            def add_part(part, carry):
                sum_ref[...] += one_part(part)
                return carry

            lax.fori_loop(1, picks[block], add_part, 0)
            out_ref[block] = sum_ref[...].astype(BF16)

        when_at(block, lambda each: save(each).start())
        return carry

    lax.fori_loop(0, blocks, sum_block, 0)
    for block in range(blocks):
        save(block).wait()


def run_experts(starts, picks, tiles, pieces, ranks, shares, own, other):
    features = pieces[0].shape[1]
    hidden = own[0].shape[1]
    blocks = ranks.shape[0]
    count = len(pieces)
    tokens = blocks * BLOCK
    capacity = tokens + max(BLOCK, tile_rows(blocks))
    anywhere = pl.BlockSpec(memory_space=pl.ANY)
    whole = pl.BlockSpec(ranks.shape, lambda *_: (0, 0, 0))
    return pl.pallas_call(
        functools.partial(expert_kernel, count),
        grid_spec=pltpu.PrefetchScalarGridSpec(
            num_scalar_prefetch=3,
            grid=(1,),
            in_specs=[anywhere] * count + [whole] * 2 + [anywhere] * 6,
            out_specs=[anywhere] * count,
            scratch_shapes=[
                pltpu.VMEM((4, capacity, features), BF16),
                pltpu.VMEM((4, hidden, features), BF16),
                pltpu.VMEM((4, hidden, features), BF16),
                pltpu.VMEM((4, hidden, features), BF16),
                pltpu.VMEM((blocks, BLOCK, features), BF16),
                pltpu.VMEM((blocks, BLOCK, features), BF16),
                pltpu.VMEM((BLOCK, features), F32),
                pltpu.SemaphoreType.DMA((blocks,)),
                pltpu.SemaphoreType.DMA((blocks,)),
                pltpu.SemaphoreType.DMA((4, 3)),
            ],
        ),
        out_shape=[jax.ShapeDtypeStruct(piece.shape, BF16) for piece in pieces],
        compiler_params=pltpu.CompilerParams(vmem_limit_bytes=56 * 1024 * 1024),
        cost_estimate=pl.CostEstimate(
            flops=8 * tokens * features * hidden, bytes_accessed=26_000_000, transcendentals=0
        ),
    )(starts, picks, tiles, *pieces, ranks, shares, *own, *other)


def body(policy_states, row_lengths, send_order, expert_ids, gate_codes, w_gate, w_up, w_down):
    features = policy_states.shape[3]
    maxlen = policy_states.shape[2]
    top = expert_ids.shape[-1]
    x, y, core = (lax.axis_index(name) for name in PLANE)
    column = (x * 4 + y) * 2 + core
    device = lax.axis_index("dp") * 32 + column
    swap = [(0, 1), (1, 0)]
    own = [jnp.swapaxes(w_gate, 1, 2), jnp.swapaxes(w_up, 1, 2), w_down]
    other = [lax.ppermute(w, "core", swap) for w in own]

    packed = jnp.concatenate([row_lengths, send_order])
    spread = lax.all_to_all(
        jnp.broadcast_to(packed[None], (32, 16)), PLANE, 0, 0, tiled=True
    )
    lengths = spread[:, :8].T.reshape(256)
    held_by = (spread[:, 8:].T * 32 + jnp.arange(32, dtype=I32)[None, :]).reshape(256)
    every = jnp.arange(256, dtype=I32)
    offsets = jnp.sum(jnp.where(every[None, :] < every[:, None], lengths[None, :], 0), axis=1)
    is_holder = held_by[:, None] == every[None, :]
    judge_offsets = jnp.sum(jnp.where(is_holder, offsets[None, :], 0), axis=1)
    judge_lengths = jnp.sum(jnp.where(is_holder, lengths[None, :], 0), axis=1)
    at_me = every == device
    mine = jnp.sum(jnp.where(at_me, offsets, 0))
    judged_at = jnp.sum(jnp.where(at_me, judge_offsets, 0))
    judged_len = jnp.sum(jnp.where(at_me, judge_lengths, 0))

    pairs = jnp.arange(2 * 256, dtype=I32)
    peer, turn = pairs // 2, pairs % 2
    positions = jnp.arange(maxlen, dtype=I32)
    sent = lambda offset: (peer - offset) % 256 + 256 * turn
    rows = pick(one_hot(sent(mine), positions), policy_states.reshape(maxlen, features))
    names = jnp.concatenate(
        [
            expert_ids.reshape(maxlen, top).astype(BF16),
            gate_codes.reshape(maxlen, top).astype(BF16),
            jnp.zeros((maxlen, 128 - 2 * top), BF16),
        ],
        axis=1,
    )
    names = pick(one_hot(sent(judged_at), positions), names)
    outbound = jnp.concatenate([rows, names], axis=1).reshape(256, 2, features + 128)
    inbound = lax.all_to_all(outbound, ALL, 0, 0, tiled=True)
    inbound, *other = together([inbound, *other])
    inbound = inbound.reshape(512, features + 128)

    def slots_of(offset, length):
        offset, length = jnp.repeat(offset, 2), jnp.repeat(length, 2)
        position = (device - offset) % 256 + 256 * turn
        return jnp.where(position < length, (offset + position) // 256, -1)

    to_slot = one_hot(every, slots_of(offsets, lengths))
    judge_slot = one_hot(every, slots_of(judge_offsets, judge_lengths))
    states = pick(to_slot, inbound[:, :features])
    named = lax.dot_general(
        inbound[:, features : features + 16], judge_slot, (((0,), (1,)), ((), ())),
        preferred_element_type=F32,
    ).astype(BF16)

    experts = jnp.stack([2 * column, 2 * column + 1, 2 * (column ^ 1), 2 * (column ^ 1) + 1])
    below = (jnp.arange(BLOCK)[:, None] < jnp.arange(BLOCK)[None, :]).astype(BF16)

    def judge(pieces, named_here):
        blocks = named_here.shape[1] // BLOCK
        codes = named_here[top : 2 * top].astype(F32)
        share = codes / jnp.sum(codes, axis=0, keepdims=True)
        hit = named_here[None, :top].astype(I32) == experts[:, None, None]
        mask = jnp.any(hit, axis=1)
        shares = jnp.sum(jnp.where(hit, share[None], 0.0), axis=1)
        mask = mask.reshape(4, blocks, BLOCK)
        rank = jnp.dot(
            mask.reshape(4 * blocks, BLOCK).astype(BF16), below, preferred_element_type=F32
        ).reshape(4, blocks, BLOCK)
        ranks = jnp.where(mask, rank, -1.0).transpose(1, 0, 2)
        shares = shares.reshape(4, blocks, BLOCK).transpose(1, 0, 2)
        count = jnp.sum(mask.astype(I32), axis=2)
        taken = (count + 15) // 16 * 16
        earlier = jnp.arange(blocks)[None, :] < jnp.arange(blocks)[:, None]
        starts = jnp.sum(jnp.where(earlier[None], taken[:, None, :], 0), axis=2)
        tile = tile_rows(blocks)
        tiles = (jnp.sum(taken, axis=1) + tile - 1) // tile
        picks = jnp.max((count + PICK - 1) // PICK, axis=0)
        return run_experts(starts.reshape(-1), picks, tiles, pieces, ranks, shares, own, other)

    lines, all_named = gather_lines(states[:128], states[128:], named)
    all_named = from_here(from_here(all_named, "x", 0), "y", 1)
    named_parts = [
        all_named[..., :128].transpose(2, 1, 0, 3).reshape(16, 4, 2, 256),
        all_named[..., 128:].transpose(2, 0, 1, 3).reshape(16, 4, 2, 256),
    ]

    def names_of(*places):
        return jnp.concatenate([named_parts[p][:, line, half] for p, line, half in places], axis=1)

    axes = "yx"
    first = together(
        [shift(lines[2 * p + half], axes[p], by) for p in range(2) for half, by in ((0, -1), (1, 1))]
    )
    far = [shift(first[2 * p + half], axes[p], by) for p in range(2) for half, by in ((0, -1), (1, 1))]
    made_first = judge(
        [*lines[:2], *first],
        names_of((0, 0, 0), (0, 0, 1), (0, 1, 0), (0, 3, 1), (1, 1, 0), (1, 3, 1)),
    )
    held = together([*far, *made_first, *lines])
    far, made_first, lines = held[:4], held[4:10], held[10:]
    second = [shift(lines[2 * p + half], axes[p], by) for p in range(2) for half, by in ((1, -1), (0, 1))]
    made_far = judge(far, names_of((0, 2, 0), (0, 2, 1), (1, 2, 0), (1, 2, 1)))
    held = together([*second, *made_far, *made_first, *lines[2:]])
    second, made_far, made_first, lines = held[:4], held[4:8], held[8:14], held[14:]
    across = [shift(made_far[2 * p + half], axes[p], by) for p in range(2) for half, by in ((0, -1), (1, 1))]
    whole = [
        shift(made_first[2 + 2 * p + half], axes[p], by) for p in range(2) for half, by in ((0, 1), (1, -1))
    ]
    made_second = judge(
        [*second, *lines],
        names_of((0, 1, 1), (0, 3, 0), (1, 1, 1), (1, 3, 0), (1, 0, 0), (1, 0, 1)),
    )
    held = together([*across, *made_second])
    across, made_second = held[:4], held[4:]
    summed = []
    for p in range(2):
        after, before = made_second[2 * p : 2 * p + 2]
        low, high = across[2 * p : 2 * p + 2]
        summed += [shift(add(before, low), axes[p], -1), shift(add(after, high), axes[p], 1)]
    held = together([*summed, *whole])
    summed, whole = held[:4], held[4:]
    stays = [made_first[:2], made_second[4:]]
    finished = last_sums(
        [add(stays[p][half], summed[2 * p + half], whole[2 * p + half]) for p in range(2) for half in range(2)]
    )

    made = jnp.concatenate(finished)
    back = lax.dot_general(
        judge_slot, made, (((0,), (0,)), ((), ())), preferred_element_type=F32
    ).astype(BF16)
    back = lax.all_to_all(back.reshape(256, 2, features), ALL, 0, 0, tiled=True)
    found = jnp.where(
        positions < judged_len, (positions + judged_at) % 256 * 2 + positions // 256, -1
    )
    result = pick(one_hot(found, pairs), back.reshape(512, features))
    return result.reshape(1, maxlen, features)


def solution(mesh):
    fine = Mesh(mesh.devices.reshape(8, 4, 4, 2), ALL)
    in_specs = (
        P(PLANE, "dp", None, None),
        P(PLANE),
        P(PLANE),
        P("dp", PLANE, None, None),
        P("dp", PLANE, None, None),
        P(PLANE, None, None),
        P(PLANE, None, None),
        P(PLANE, None, None),
    )
    return jax.shard_map(
        body, mesh=fine, in_specs=in_specs, out_specs=P(ALL, None, None), check_vma=False
    )
```

```python
import functools

import jax
import jax.numpy as jnp
from jax import lax
from jax.experimental import pallas as pl
from jax.experimental.pallas import tpu as pltpu
from jax.sharding import Mesh, PartitionSpec as P

F32 = jnp.float32
BF16 = jnp.bfloat16
I32 = jnp.int32
ALL = ("dp", "x", "y", "core")
PLANE = ("x", "y", "core")
BLOCK = 256
PICK = 64


def one_hot(rows, columns):
    return (rows[:, None] == columns[None, :]).astype(BF16)


def pick(matrix, values):
    return jnp.dot(matrix, values, preferred_element_type=F32).astype(BF16)


def shift(value, axis, by):
    size = lax.axis_size(axis)
    return lax.ppermute(value, axis, [(i, (i + by) % size) for i in range(size)])


def together(values):
    return list(lax.optimization_barrier(tuple(values)))


def add(*values):
    return sum(value.astype(F32) for value in values).astype(BF16)


def gather_lines(one, two, named):
    steps = (-1, -2, 1)
    lines = [shift(one, "x", by) for by in steps] + [shift(two, "y", by) for by in steps]
    lines[0], named = together([lines[0], named])
    named = lax.all_to_all(
        jnp.broadcast_to(named[None], (16, *named.shape)), ("x", "y"), 0, 0, tiled=True
    ).reshape(4, 4, *named.shape)
    lines = together(lines)
    halves = together(
        [
            jnp.concatenate(pair)
            for pair in ((one, lines[0]), lines[1:3], (two, lines[3]), lines[4:6])
        ]
    )
    return halves, named


def last_sums(lines):
    size = lines[0].shape[0] // 2
    cut = together([line[i * size : (i + 1) * size] for line in lines for i in range(2)])
    found = together(
        [
            shift(cut[4 * j + i], axis, by)
            for j, axis in enumerate("xy")
            for i, by in ((1, 1), (2, 2), (3, -1))
        ]
    )
    return [add(cut[0], *found[:3]), add(cut[4], *found[3:])]


def from_here(value, axis, dim):
    twice = jnp.concatenate([value, value], dim)
    return lax.dynamic_slice_in_dim(twice, lax.axis_index(axis), value.shape[dim], dim)


def tile_rows(blocks):
    return (blocks * 36 + 15) // 16 * 16


def expert_kernel(count, starts, picks, tiles, *refs):
    pieces, (ranks, shares), weights, outs, scratch = (
        refs[:count], refs[count : count + 2], refs[count + 2 : count + 8],
        refs[count + 8 : 2 * count + 8], refs[2 * count + 8 :],
    )
    gate0, up0, down0, gate1, up1, down1 = weights
    rows_ref, gate_ref, up_ref, down_ref, in_ref, out_ref, sum_ref = scratch[:7]
    in_sems, out_sems, w_sems = scratch[7:]
    blocks = ranks.shape[0]

    tile = tile_rows(blocks)
    spots = [(i, at) for i in range(count) for at in range(pieces[i].shape[0] // BLOCK)]

    def part_of(refs, block):
        piece, at = spots[block]
        return refs[piece].at[pl.ds(at * BLOCK, BLOCK)]

    def load(block):
        return pltpu.make_async_copy(part_of(pieces, block), in_ref.at[block], in_sems.at[block])

    def save(block):
        return pltpu.make_async_copy(out_ref.at[block], part_of(outs, block), out_sems.at[block])

    def when_at(block, action):
        for each in range(blocks):
            pl.when(block == each)(functools.partial(action, each))

    def weight_copies(expert):
        gate, up, down = ((gate0, up0, down0), (gate1, up1, down1))[expert // 2]
        return [
            pltpu.make_async_copy(w.at[expert % 2], ref.at[expert], w_sems.at[expert, i])
            for i, (w, ref) in enumerate(((gate, gate_ref), (up, up_ref), (down, down_ref)))
        ]

    def mask_of(block, part):
        lane_rank = ranks[block]
        wanted = (lax.broadcasted_iota(I32, (PICK, BLOCK), 0) + part * PICK).astype(F32)
        return [jnp.where(lane_rank[e : e + 1, :] == wanted, 1.0, 0.0) for e in range(4)]

    def place(expert, block, part):
        return pl.ds(pl.multiple_of(starts[expert * blocks + block] + part * PICK, 16), PICK)

    for block in range(blocks):
        load(block).start()

    def fetch(expert):
        for copy in weight_copies(expert):
            copy.start()

    def pick_block(block, carry):
        when_at(block, lambda each: load(each).wait())
        pl.when(block == 0)(functools.partial(fetch, 0))
        pl.when(block == blocks // 2)(functools.partial(fetch, 1))

        def one_part(part, carry):
            mask = jnp.concatenate(mask_of(block, part)).astype(BF16)
            got = jnp.dot(mask, in_ref[block], preferred_element_type=F32).astype(BF16)
            for e in range(4):
                rows_ref[e, place(e, block, part), :] = got[e * PICK : (e + 1) * PICK]
            return carry

        one_part(0, 0)
        return lax.fori_loop(1, picks[block], one_part, carry)

    lax.fori_loop(0, blocks, pick_block, 0)

    for expert in range(4):
        if expert < 2:
            fetch(expert + 2)
        for copy in weight_copies(expert):
            copy.wait()

        def one_tile(i, carry, expert=expert):
            at = pl.ds(pl.multiple_of(i * tile, 16), tile)
            held = rows_ref[expert, at, :]
            turned = (((1,), (1,)), ((), ()))
            gated = lax.dot_general(held, gate_ref[expert], turned, preferred_element_type=F32)
            raised = lax.dot_general(held, up_ref[expert], turned, preferred_element_type=F32)
            hidden = (gated / (1.0 + jnp.exp(-gated)) * raised).astype(BF16)
            rows_ref[expert, at, :] = jnp.dot(
                hidden, down_ref[expert], preferred_element_type=F32
            ).astype(BF16)
            return carry

        lax.fori_loop(0, tiles[expert], one_tile, 0)

    def sum_block(block, carry):
        share = shares[block]

        def one_part(part):
            masks = mask_of(block, part)
            weight = jnp.concatenate([masks[e] * share[e : e + 1, :] for e in range(4)])
            high = weight.astype(BF16)
            low = (weight - high.astype(F32)).astype(BF16)
            made = jnp.concatenate([rows_ref[e, place(e, block, part), :] for e in range(4)])
            dims = (((0,), (0,)), ((), ()))
            return lax.dot_general(
                high, made, dims, preferred_element_type=F32
            ) + lax.dot_general(low, made, dims, preferred_element_type=F32)

        out_ref[block] = one_part(0).astype(BF16)

        @pl.when(picks[block] > 1)
        def _():
            sum_ref[...] = one_part(0)

            def add_part(part, carry):
                sum_ref[...] += one_part(part)
                return carry

            lax.fori_loop(1, picks[block], add_part, 0)
            out_ref[block] = sum_ref[...].astype(BF16)

        when_at(block, lambda each: save(each).start())
        return carry

    lax.fori_loop(0, blocks, sum_block, 0)
    for block in range(blocks):
        save(block).wait()


def run_experts(starts, picks, tiles, pieces, ranks, shares, own, other):
    features = pieces[0].shape[1]
    hidden = own[0].shape[1]
    blocks = ranks.shape[0]
    count = len(pieces)
    tokens = blocks * BLOCK
    capacity = tokens + max(BLOCK, tile_rows(blocks))
    anywhere = pl.BlockSpec(memory_space=pl.ANY)
    whole = pl.BlockSpec(ranks.shape, lambda *_: (0, 0, 0))
    return pl.pallas_call(
        functools.partial(expert_kernel, count),
        grid_spec=pltpu.PrefetchScalarGridSpec(
            num_scalar_prefetch=3,
            grid=(1,),
            in_specs=[anywhere] * count + [whole] * 2 + [anywhere] * 6,
            out_specs=[anywhere] * count,
            scratch_shapes=[
                pltpu.VMEM((4, capacity, features), BF16),
                pltpu.VMEM((4, hidden, features), BF16),
                pltpu.VMEM((4, hidden, features), BF16),
                pltpu.VMEM((4, hidden, features), BF16),
                pltpu.VMEM((blocks, BLOCK, features), BF16),
                pltpu.VMEM((blocks, BLOCK, features), BF16),
                pltpu.VMEM((BLOCK, features), F32),
                pltpu.SemaphoreType.DMA((blocks,)),
                pltpu.SemaphoreType.DMA((blocks,)),
                pltpu.SemaphoreType.DMA((4, 3)),
            ],
        ),
        out_shape=[jax.ShapeDtypeStruct(piece.shape, BF16) for piece in pieces],
        compiler_params=pltpu.CompilerParams(vmem_limit_bytes=56 * 1024 * 1024),
        cost_estimate=pl.CostEstimate(
            flops=8 * tokens * features * hidden, bytes_accessed=26_000_000, transcendentals=0
        ),
    )(starts, picks, tiles, *pieces, ranks, shares, *own, *other)


def body(policy_states, row_lengths, send_order, expert_ids, gate_codes, w_gate, w_up, w_down):
    features = policy_states.shape[3]
    maxlen = policy_states.shape[2]
    top = expert_ids.shape[-1]
    x, y, core = (lax.axis_index(name) for name in PLANE)
    column = (x * 4 + y) * 2 + core
    device = lax.axis_index("dp") * 32 + column
    swap = [(0, 1), (1, 0)]
    own = [jnp.swapaxes(w_gate, 1, 2), jnp.swapaxes(w_up, 1, 2), w_down]
    other = [lax.ppermute(w, "core", swap) for w in own]

    packed = jnp.concatenate([row_lengths, send_order])
    spread = lax.all_to_all(
        jnp.broadcast_to(packed[None], (32, 16)), PLANE, 0, 0, tiled=True
    )
    lengths = spread[:, :8].T.reshape(256)
    held_by = (spread[:, 8:].T * 32 + jnp.arange(32, dtype=I32)[None, :]).reshape(256)
    every = jnp.arange(256, dtype=I32)
    offsets = jnp.sum(jnp.where(every[None, :] < every[:, None], lengths[None, :], 0), axis=1)
    is_holder = held_by[:, None] == every[None, :]
    judge_offsets = jnp.sum(jnp.where(is_holder, offsets[None, :], 0), axis=1)
    judge_lengths = jnp.sum(jnp.where(is_holder, lengths[None, :], 0), axis=1)
    at_me = every == device
    mine = jnp.sum(jnp.where(at_me, offsets, 0))
    judged_at = jnp.sum(jnp.where(at_me, judge_offsets, 0))
    judged_len = jnp.sum(jnp.where(at_me, judge_lengths, 0))

    pairs = jnp.arange(2 * 256, dtype=I32)
    peer, turn = pairs // 2, pairs % 2
    positions = jnp.arange(maxlen, dtype=I32)
    sent = lambda offset: (peer - offset) % 256 + 256 * turn
    rows = pick(one_hot(sent(mine), positions), policy_states.reshape(maxlen, features))
    names = jnp.concatenate(
        [
            expert_ids.reshape(maxlen, top).astype(BF16),
            gate_codes.reshape(maxlen, top).astype(BF16),
            jnp.zeros((maxlen, 128 - 2 * top), BF16),
        ],
        axis=1,
    )
    names = pick(one_hot(sent(judged_at), positions), names)
    outbound = jnp.concatenate([rows, names], axis=1).reshape(256, 2, features + 128)
    inbound = lax.all_to_all(outbound, ALL, 0, 0, tiled=True)
    inbound, *other = together([inbound, *other])
    inbound = inbound.reshape(512, features + 128)

    def slots_of(offset, length):
        offset, length = jnp.repeat(offset, 2), jnp.repeat(length, 2)
        position = (device - offset) % 256 + 256 * turn
        return jnp.where(position < length, (offset + position) // 256, -1)

    to_slot = one_hot(every, slots_of(offsets, lengths))
    judge_slot = one_hot(every, slots_of(judge_offsets, judge_lengths))
    states = pick(to_slot, inbound[:, :features])
    named = lax.dot_general(
        inbound[:, features : features + 16], judge_slot, (((0,), (1,)), ((), ())),
        preferred_element_type=F32,
    ).astype(BF16)

    experts = jnp.stack([2 * column, 2 * column + 1, 2 * (column ^ 1), 2 * (column ^ 1) + 1])
    below = (jnp.arange(BLOCK)[:, None] < jnp.arange(BLOCK)[None, :]).astype(BF16)

    def judge(pieces, named_here):
        blocks = named_here.shape[1] // BLOCK
        codes = named_here[top : 2 * top].astype(F32)
        share = codes / jnp.sum(codes, axis=0, keepdims=True)
        hit = named_here[None, :top].astype(I32) == experts[:, None, None]
        mask = jnp.any(hit, axis=1)
        shares = jnp.sum(jnp.where(hit, share[None], 0.0), axis=1)
        mask = mask.reshape(4, blocks, BLOCK)
        rank = jnp.dot(
            mask.reshape(4 * blocks, BLOCK).astype(BF16), below, preferred_element_type=F32
        ).reshape(4, blocks, BLOCK)
        ranks = jnp.where(mask, rank, -1.0).transpose(1, 0, 2)
        shares = shares.reshape(4, blocks, BLOCK).transpose(1, 0, 2)
        count = jnp.sum(mask.astype(I32), axis=2)
        taken = (count + 15) // 16 * 16
        earlier = jnp.arange(blocks)[None, :] < jnp.arange(blocks)[:, None]
        starts = jnp.sum(jnp.where(earlier[None], taken[:, None, :], 0), axis=2)
        tile = tile_rows(blocks)
        tiles = (jnp.sum(taken, axis=1) + tile - 1) // tile
        picks = jnp.max((count + PICK - 1) // PICK, axis=0)
        return run_experts(starts.reshape(-1), picks, tiles, pieces, ranks, shares, own, other)

    lines, all_named = gather_lines(states[:128], states[128:], named)
    all_named = from_here(from_here(all_named, "x", 0), "y", 1)
    named_parts = [
        all_named[..., :128].transpose(2, 1, 0, 3).reshape(16, 4, 2, 256),
        all_named[..., 128:].transpose(2, 0, 1, 3).reshape(16, 4, 2, 256),
    ]

    def names_of(*places):
        return jnp.concatenate([named_parts[p][:, line, half] for p, line, half in places], axis=1)

    axes = "yx"
    first = together(
        [shift(lines[2 * p + half], axes[p], by) for p in range(2) for half, by in ((0, -1), (1, 1))]
    )
    far = [shift(first[2 * p + half], axes[p], by) for p in range(2) for half, by in ((0, -1), (1, 1))]
    made_first = judge(
        [*lines[:2], *first],
        names_of((0, 0, 0), (0, 0, 1), (0, 1, 0), (0, 3, 1), (1, 1, 0), (1, 3, 1)),
    )
    held = together([*far, *made_first, *lines])
    far, made_first, lines = held[:4], held[4:10], held[10:]
    second = [shift(lines[2 * p + half], axes[p], by) for p in range(2) for half, by in ((1, -1), (0, 1))]
    early = shift(made_first[3], "y", -1)
    made_far = judge(far, names_of((0, 2, 0), (0, 2, 1), (1, 2, 0), (1, 2, 1)))
    held = together([*second, *made_far, *made_first, *lines[2:], early])
    second, made_far, made_first, lines = held[:4], held[4:8], held[8:14], held[14:16]
    early = held[16]
    across = [shift(made_far[2 * p + half], axes[p], by) for p in range(2) for half, by in ((0, -1), (1, 1))]
    whole = [
        shift(made_first[2], "y", 1), early, shift(made_first[4], "x", 1), shift(made_first[5], "x", -1)
    ]
    made_second = judge(
        [*second, *lines],
        names_of((0, 1, 1), (0, 3, 0), (1, 1, 1), (1, 3, 0), (1, 0, 0), (1, 0, 1)),
    )
    held = together([*across, whole[2], *made_second])
    across, whole[2], made_second = held[:4], held[4], held[5:]
    summed = []
    for p in range(2):
        after, before = made_second[2 * p : 2 * p + 2]
        low, high = across[2 * p : 2 * p + 2]
        summed += [shift(add(before, low), axes[p], -1), shift(add(after, high), axes[p], 1)]
    held = together([*summed, *whole])
    summed, whole = held[:4], held[4:]
    stays = [made_first[:2], made_second[4:]]
    finished = last_sums(
        [add(stays[p][half], summed[2 * p + half], whole[2 * p + half]) for p in range(2) for half in range(2)]
    )

    made = jnp.concatenate(finished)
    back = lax.dot_general(
        judge_slot, made, (((0,), (0,)), ((), ())), preferred_element_type=F32
    ).astype(BF16)
    back = lax.all_to_all(back.reshape(256, 2, features), ALL, 0, 0, tiled=True)
    found = jnp.where(
        positions < judged_len, (positions + judged_at) % 256 * 2 + positions // 256, -1
    )
    result = pick(one_hot(found, pairs), back.reshape(512, features))
    return result.reshape(1, maxlen, features)


def solution(mesh):
    fine = Mesh(mesh.devices.reshape(8, 4, 4, 2), ALL)
    in_specs = (
        P(PLANE, "dp", None, None),
        P(PLANE),
        P(PLANE),
        P("dp", PLANE, None, None),
        P("dp", PLANE, None, None),
        P(PLANE, None, None),
        P(PLANE, None, None),
        P(PLANE, None, None),
    )
    return jax.shard_map(
        body, mesh=fine, in_specs=in_specs, out_specs=P(ALL, None, None), check_vma=False
    )
```
